32 devices in a mesh: groups: 2 (over y), tile: 4 (over z), sect: 4 (over x, core).
Axes of the slice: x: 2, y: 2, z: 4, core: 2. Of those that a mesh axis runs over, the one named last changes fastest.
Arguments:
- labels: int32 [16, 128, 512], P(('groups', 'sect'), None, 'tile'), parts along dimension 0, may hold values from 0 to 15
- classes: int32 [16, 128, 512], P(('groups', 'sect'), None, 'tile'), parts along dimension 0, may hold values from 0 to 7
- positions: int32 [8], P('groups'), parts along dimension 0, may hold values from 0 to 127
- phase_table: float32 [8], replicated, may hold values from -3.140625 to 3.140625
- brightness: float32 [16], replicated, may hold values from 0.2 to 2
- prop_taps: float32 [2, 2, 129], replicated, may hold values from -1 to 1, as said below
- detect_taps: float32 [2, 129], replicated, may hold values from 0 to 1, as said below
Outputs:
- image: float32 [16, 128, 512], P(('groups', 'sect'), None, 'tile'), parts along dimension 0
The draws below stay inside these ranges and needn't reach their ends.
There are 2 independent parts, one for each index of `groups`. The reference program is written for one: setup_inputs(seed, part) draws one part's arguments, and reference() takes and returns one part's arrays. A program takes and returns all parts, laid end to end along the dimension named above; an argument that names none is the same for every part. Nothing has to cross between parts.
Inputs may be any that keep to these rules, and one draw needn't show every extreme that they name: `prop_taps`: the squares of the 2 x 129 entries of each axis's propagation taps sum to 1. `detect_taps`: each axis's detection taps are positive and sum to 1.
All inputs are finite; a program needn't handle non-finite values.
Results may differ from the reference program's by a relative error of at most 0.0001.
Values sent between devices are 32-bit elements; how exact they have to be, the bound alone decides.
No kernel may reach another device: no remote copies, remote signals or barrier semaphores. Data moves between devices by JAX's collectives and lax.ppermute only.
A program may use at most 64 MiB of HBM per device.

```python
import math
import jax
import jax.numpy as jnp
from jax import lax

TAPS = 129
RCLASS = 8
LABELS = 16
NY = 128
CZ = 128
POSITIONS = 4
NX = 8
NZ = 512


def draw_prop_taps(key, part):
    raw = jax.random.normal(key, (2, 2, TAPS), jnp.float32)
    scale = jnp.sqrt(jnp.sum(raw * raw, axis=(1, 2), keepdims=True))
    return raw / scale


def draw_detect_taps(key, part):
    raw = jax.random.uniform(key, (2, TAPS), jnp.float32, 0.1, 1.0)
    middle = (lax.broadcasted_iota(jnp.int32, (2, TAPS), 1) == TAPS // 2).astype(jnp.float32)
    raw = raw + middle * jnp.sum(raw, axis=1, keepdims=True)
    return raw / jnp.sum(raw, axis=1, keepdims=True)


def with_ends(entries, key, smallest, high):
    longest = entries.shape.index(max(entries.shape))
    spots = []
    for shift in (0, 1):
        where = [jax.random.randint(jax.random.fold_in(key, axis), (), 0, length) for axis, length in enumerate(entries.shape)]
        where[longest] = (where[longest] + shift) % entries.shape[longest]
        spots.append(tuple(where))
    return entries.at[spots[0]].set(smallest).at[spots[1]].set(high)


def setup_inputs(seed: int = 0, part: int = 0) -> dict:
    key_of = jax.random.split(jax.random.key(seed), 8)
    own_keys = jax.random.split(jax.random.fold_in(key_of[7], part), 8)
    return {
        "labels": with_ends(jax.random.randint(own_keys[0], (NX, NY, NZ), 0, LABELS), jax.random.fold_in(own_keys[0], 1), 0, LABELS - 1).astype(jnp.int32),
        "classes": with_ends(jax.random.randint(own_keys[1], (NX, NY, NZ), 0, RCLASS), jax.random.fold_in(own_keys[1], 1), 0, RCLASS - 1).astype(jnp.int32),
        "positions": with_ends(jax.random.randint(own_keys[2], (POSITIONS,), 0, NY), jax.random.fold_in(own_keys[2], 1), 0, NY - 1).astype(jnp.int32),
        "phase_table": jnp.clip(jax.random.uniform(key_of[3], (RCLASS,), jnp.float32, -3.140625, 3.140625), -3.140625, 3.140625),
        "brightness": jnp.clip(jnp.exp(jax.random.uniform(key_of[4], (LABELS,), jnp.float32, math.log(0.2), math.log(2.0))), 0.2, 2.0),
        "prop_taps": draw_prop_taps(jax.random.fold_in(key_of[7], 71), part),
        "detect_taps": draw_detect_taps(jax.random.fold_in(key_of[7], 71), part),
    }


SHEET_WIDTH = 6.0
AMPLITUDE = 2.0


def toeplitz(tap_rows, size_in, size_out, shift, period):
    count = tap_rows.shape[-1]
    inner = lax.broadcasted_iota(jnp.int32, (size_in, size_out), 0)
    outer = lax.broadcasted_iota(jnp.int32, (size_in, size_out), 1)
    offset = inner - outer + shift
    if period > 0:
        tap_place = lax.broadcasted_iota(jnp.int32, (count, period), 0)
        target = lax.broadcasted_iota(jnp.int32, (count, period), 1)
        folding = (jnp.mod(tap_place, period) == target).astype(tap_rows.dtype)
        table = jnp.einsum("...t,tj->...j", tap_rows, folding, precision=lax.Precision.HIGHEST)
        index = jnp.mod(offset, period).astype(jnp.int32)
        return jnp.take(table, index, axis=-1)
    index = jnp.clip(offset, 0, count - 1).astype(jnp.int32)
    valid = (offset >= 0) & (offset < count)
    values = jnp.take(tap_rows, index, axis=-1)
    return jnp.where(valid, values, jnp.zeros_like(values))


def complex_block(parts):
    real_part, imag_part = parts[0], parts[1]
    return jnp.stack([jnp.stack([real_part, imag_part]), jnp.stack([-imag_part, real_part])])


def lookup(indices, table):
    total = jnp.zeros(indices.shape, jnp.float32)
    for entry in range(table.shape[0]):
        total = total + jnp.where(indices == entry, table[entry], 0.0)
    return total


def sheet_plane(position, y_cells, z_cells):
    place = lax.broadcasted_iota(jnp.int32, (y_cells, z_cells), 0).astype(jnp.float32)
    offset = (place - position.astype(jnp.float32)) / SHEET_WIDTH
    real_part = AMPLITUDE * jnp.exp(-offset * offset)
    return jnp.stack([real_part, jnp.zeros_like(real_part)])


def apply_phase(field, cosine, sine):
    real_part = field[..., 0, :, :]
    imag_part = field[..., 1, :, :]
    return jnp.stack([real_part * cosine - imag_part * sine, real_part * sine + imag_part * cosine], axis=-3)


def along_y(field, y_band):
    return jnp.einsum("cdio,...ciz->...doz", y_band, field, precision=lax.Precision.HIGHEST, preferred_element_type=jnp.float32)


def windows_of(field, block, half_taps):
    z_cells = field.shape[-1]
    widths = [(0, 0)] * (field.ndim - 1) + [(half_taps, half_taps)]
    padded = jnp.pad(field, widths)
    pieces = [padded[..., number * block: number * block + block + 2 * half_taps] for number in range(z_cells // block)]
    return jnp.stack(pieces, axis=-2)


def reference(labels, classes, positions, phase_table, brightness, prop_taps, detect_taps):
    x_cells, y_cells, z_cells = labels.shape
    half_taps = prop_taps.shape[-1] // 2
    cosine = lookup(classes, jnp.cos(phase_table))
    sine = lookup(classes, jnp.sin(phase_table))
    y_band = complex_block(toeplitz(prop_taps[0], y_cells, y_cells, half_taps, y_cells))
    z_band = complex_block(toeplitz(prop_taps[1], CZ + 2 * half_taps, CZ, 0, 0))

    def advance(field, maps):
        field = apply_phase(field, maps[0], maps[1])
        field = along_y(field, y_band)
        windows = windows_of(field, CZ, half_taps)
        field = jnp.einsum("cybi,cdio->dybo", windows, z_band, precision=lax.Precision.HIGHEST, preferred_element_type=jnp.float32)
        field = field.reshape(2, y_cells, z_cells)
        return field, field[0] * field[0] + field[1] * field[1]

    collected = jnp.zeros(labels.shape, jnp.float32)
    for number in range(POSITIONS):
        start = sheet_plane(positions[number], y_cells, z_cells)
        _, left_power = lax.scan(advance, start, (cosine, sine))
        _, right_power = lax.scan(advance, start, (cosine, sine), reverse=True)
        collected = collected + left_power + right_power
    excitation = lookup(labels, brightness) * collected
    blur_y = toeplitz(detect_taps[0], y_cells, y_cells, half_taps, y_cells)
    blurred = jnp.einsum("io,xiz->xoz", blur_y, excitation, precision=lax.Precision.HIGHEST, preferred_element_type=jnp.float32)
    blur_z = toeplitz(detect_taps[1], CZ + 2 * half_taps, CZ, 0, 0)
    windows = windows_of(blurred, CZ, half_taps)
    image = jnp.einsum("xybi,io->xybo", windows, blur_z, precision=lax.Precision.HIGHEST, preferred_element_type=jnp.float32)
    return image.reshape(x_cells, y_cells, z_cells)
```

```python
import functools

import jax
import jax.numpy as jnp
from jax import lax
from jax.experimental import pallas as pl
from jax.experimental.pallas import tpu as pltpu
from jax.sharding import PartitionSpec as P

SHEET_WIDTH = 6.0
AMPLITUDE = 2.0
VMEM_BYTES = 48 * 1024 * 1024
SMEM = pltpu.SMEM
VMEM = pltpu.VMEM


class Plan:
    def __init__(self, labels, positions, taps):
        self.planes, self.ny, self.cz = labels.shape
        self.half = taps // 2
        self.taps = taps
        self.tiles = lax.axis_size("tile")
        self.sections = lax.axis_size("sect")
        self.tile = lax.axis_index("tile")
        self.sect = lax.axis_index("sect")
        self.cores = self.sections // 2
        self.core = self.sect % self.cores
        self.side = self.sect // self.cores
        self.own = self.cores * self.planes
        self.all_x = 2 * self.own
        self.sheets = -(-positions // self.cores)
        self.block = 2 * self.half
        self.units = self.cz // self.half
        self.reach = -(-(self.all_x + 1) * self.half // self.cz)
        self.whole = self.tiles <= 2 * self.reach + 1
        self.window = self.tiles if self.whole else 2 * self.reach + 1
        self.rows = self.window * self.cz
        self.extent = self.cz + 2 * self.half

    def span(self, left):
        need = self.units + 2 + 2 * left
        if self.whole:
            width = min(need, self.window * self.units)
            start = jnp.clip(self.tile * self.units - 1 - left, 0, self.window * self.units - width)
        else:
            width = need
            start = jnp.int32(self.reach * self.units - 1 - left)
        return start, width // 2

    def home(self):
        if self.whole:
            return self.tile * self.cz
        return jnp.int32(self.reach * self.cz)


def swap(x, axis, bits):
    count = lax.axis_size(axis)
    return lax.ppermute(x, axis, [(i, i ^ bits) for i in range(count)])


def shift(x, axis, step):
    count = lax.axis_size(axis)
    return lax.ppermute(x, axis, [(i, i + step) for i in range(count) if 0 <= i + step < count])


def tile_pieces(plan, mine):
    one = jnp.int32(1)
    if plan.whole and plan.tiles & (plan.tiles - 1) == 0:
        got = {0: mine}
        if plan.tiles == 4:
            got[3] = swap(mine, "tile", 3)
            got[1] = swap(mine, "tile", 1)
            got[2] = swap(got[3], "tile", 1)
        else:
            for bits in range(1, plan.tiles):
                got[bits] = swap(mine, "tile", bits)
        return [(got[bits], plan.tile ^ bits, one) for bits in sorted(got)]
    if plan.whole:
        count = plan.tiles
        pieces = [(mine, plan.tile, one)]
        for step in range(1, count):
            turned = lax.ppermute(mine, "tile", [(i, (i + step) % count) for i in range(count)])
            pieces.append((turned, (plan.tile - step) % count, one))
        return pieces
    pieces = []
    for step in range(-plan.reach, plan.reach + 1):
        source = plan.tile + step
        valid = ((source >= 0) & (source < plan.tiles)).astype(jnp.int32)
        piece = mine if step == 0 else shift(mine, "tile", -step)
        pieces.append((piece, jnp.int32(step + plan.reach), valid))
    return pieces


def halves(x):
    high = x.astype(jnp.bfloat16)
    return high, (x - high.astype(jnp.float32)).astype(jnp.bfloat16)


def dot(a, b):
    return jnp.dot(a, b, preferred_element_type=jnp.float32)


def three(high, low, matrix_high, matrix_low):
    return dot(high, matrix_high) + dot(low, matrix_high) + dot(high, matrix_low)


def circulant(row, size, half):
    wide = jnp.broadcast_to(row, (size, size))
    return pltpu.roll(wide, (size - half) % size, 1, stride=1, stride_axis=0).T


def band(row, size, wide):
    return pltpu.roll(jnp.broadcast_to(row, (size, wide)), 0, 1, stride=1, stride_axis=0)


def prepare_kernel(ny, half, taps, dtaps, ky, kz, by, bz, line):
    block = 2 * half
    wide = 4 * half
    count = taps.shape[2]

    def padded(row):
        line[...] = jnp.zeros(line.shape, jnp.float32)
        line[0:1, :count] = row
        return line[0:1, :]

    def folded(row):
        spread = padded(row)
        return sum(spread[:, i:i + ny] for i in range(0, spread.shape[1], ny))

    def keep(ref, matrix, place=()):
        ref[(0, *place)], ref[(1, *place)] = halves(matrix)

    cyr = circulant(folded(taps[0, 0:1, :]), ny, half)
    cyi = circulant(folded(taps[0, 1:2, :]), ny, half)
    keep(ky, complex_matrix(cyr, cyi, -cyi))
    czr = band(padded(taps[1, 0:1, :])[:, :wide], block, wide)
    czi = band(padded(taps[1, 1:2, :])[:, :wide], block, wide)
    early = complex_matrix(czr[:, :block], -czi[:, :block], czi[:, :block])
    late = complex_matrix(czr[:, block:], -czi[:, block:], czi[:, block:])
    for number, matrix in enumerate((early, early + late, late)):
        keep(kz, matrix, (number,))
    keep(by, circulant(folded(dtaps[0:1, :]), ny, half))
    keep(bz, band(padded(dtaps[1:2, :])[:, :wide], block, wide))


def complex_matrix(diagonal, upper, lower):
    top = jnp.concatenate([diagonal, upper], axis=1)
    return jnp.concatenate([top, jnp.concatenate([lower, diagonal], axis=1)], axis=0)


def fill_weight(half, before, after, even, bright, labels, near, far, weight):
    def bright_of(x):
        total = jnp.zeros(x.shape, jnp.float32)
        for entry in range(bright.shape[0]):
            total = jnp.where(x == entry, bright[entry], total)
        return total

    for plane in range(labels.shape[0]):
        one, two = near[plane], far[plane]
        left = jnp.where(even, two, one)
        right = jnp.where(even, one, two)
        weight[plane, :half, :] = (bright_of(left) * before).T
        weight[plane, half:half + labels.shape[2], :] = bright_of(labels[plane]).T
        weight[plane, half + labels.shape[2]:, :] = (bright_of(right) * after).T


def beams_kernel(plan, blocks, count, total, scal, positions, table, bright, ky, kz, *refs):
    pieces = refs[:count]
    if total > plan.own:
        earlier, labels, facing, beyond, out, weight, cosine, sine, field, spread = refs[count:]
        before, after = scal[2].astype(jnp.float32), scal[3].astype(jnp.float32)
        fill_weight(plan.half, before, after, scal[4] == 0, bright, labels, facing, beyond, weight)
    else:
        out, cosine, sine, field, spread = refs[count:]
    ny, cz, half, block = plan.ny, plan.cz, plan.half, plan.block
    sheets, own, rows = plan.sheets, plan.own, plan.rows
    side = scal[0]
    home = pl.multiple_of(scal[1], half)
    first = scal.shape[0] - len(blocks)
    width = sheets * ny

    for number, piece in enumerate(pieces):
        where = scal[6 + 3 * number]
        row = pl.multiple_of(scal[7 + 3 * number] * cz, cz)
        valid = scal[8 + 3 * number] > 0
        for plane in range(plan.planes):
            kind = piece[plane].T
            bits = [(kind & 1) != 0, (kind & 2) != 0, (kind & 4) != 0]
            for part, target in ((0, cosine), (1, sine)):
                values = [jnp.where(valid, table[part, entry], 0.0) for entry in range(table.shape[1])]
                for bit in bits:
                    values = [
                        jnp.where(bit, values[i + 1], values[i]) for i in range(0, len(values), 2)
                    ]
                target[where + plane, pl.ds(row, cz), :] = values[0]

    lane = lax.broadcasted_iota(jnp.int32, (1, ny), 1).astype(jnp.float32)
    sheet = []
    for p in range(sheets):
        number = scal[5] * sheets + p
        live = number < positions.shape[0]
        centre = positions[jnp.where(live, number, 0)].astype(jnp.float32)
        offset = (lane - centre) / SHEET_WIDTH
        sheet.append(jnp.where(live, AMPLITUDE, 0.0) * jnp.exp(-offset * offset))
    field[0, half:half + rows, :] = jnp.broadcast_to(jnp.concatenate(sheet, axis=1), (rows, width))
    field[1, half:half + rows, :] = jnp.zeros((rows, width), jnp.float32)
    for ref in (field, spread):
        for d in range(2):
            ref[d, :half, :] = jnp.zeros((half, width), jnp.float32)
            ref[d, half + rows:, :] = jnp.zeros((half, width), jnp.float32)

    def each(number, body):
        if plan.whole:
            for b in range(number):
                body(b)
        else:
            lax.fori_loop(0, number, lambda b, _: body(b), None)

    def advance(slot, left, sources, targets):
        source = scal[first + left + 1] * half
        target = scal[first + left] * half

        def turn(b):
            row = pl.multiple_of(source + b * block, half)
            cos, sin = cosine[slot, pl.ds(row, block), :], sine[slot, pl.ds(row, block), :]
            parts = []
            for p in range(sheets):
                lanes = slice(p * ny, (p + 1) * ny)
                re = field[0, pl.ds(row + half, block), lanes]
                im = field[1, pl.ds(row + half, block), lanes]
                parts.append(jnp.concatenate([re * cos - im * sin, re * sin + im * cos], axis=1))
            high, low = halves(jnp.concatenate(parts, axis=0))
            v = three(high, low, ky[0], ky[1])
            for d in range(2):
                spread[d, pl.ds(row + half, block), :] = jnp.concatenate(
                    [v[p * block:(p + 1) * block, d * ny:(d + 1) * ny] for p in range(sheets)], axis=1
                )

        def product(number, x):
            high, low = halves(x)
            return dot(kz[0, number], high) + dot(kz[1, number], high) + dot(kz[0, number], low)

        def window(row):
            return jnp.concatenate([spread[d, pl.ds(row, block), :] for d in range(2)], axis=0)

        def store(row, w):
            field[0, pl.ds(row + half, block), :] = w[:block]
            field[1, pl.ds(row + half, block), :] = w[block:]

        def pair(b):
            row = pl.multiple_of(target + 2 * b * block, half)
            x = [window(row + i * block) for i in range(3)]
            middle = product(1, x[1])
            store(row, product(0, x[0] - x[1]) + middle)
            store(row + block, product(2, x[2] - x[1]) + middle)

        def single(b):
            row = pl.multiple_of(target + b * block, half)
            store(row, product(0, window(row)) + product(2, window(row + block)))

        each(sources, turn)
        each(targets // 2, pair)
        if targets % 2:
            single(targets - 1)

    def deposit(slot):
        re = field[0, pl.ds(home, plan.extent), :]
        im = field[1, pl.ds(home, plan.extent), :]
        energy = re * re + im * im
        gathered = energy[:, :ny]
        for p in range(1, sheets):
            gathered = gathered + energy[:, p * ny:(p + 1) * ny]
        out[slot] = earlier[slot] + gathered if total > own else gathered

    forward = (side == 0) if total == own else (side != 0)

    def step(k, sources, targets):
        inner = k % own
        slot = jnp.where(forward, inner, own - 1 - inner)
        left = total - 1 - k
        near = k >= total - own
        advance(slot + jnp.where(near, 0, own), left, sources, targets)

        @pl.when(near)
        def _():
            deposit(slot)

    k = 0
    while k < total:
        shape = (blocks[total - k], blocks[total - 1 - k])
        end = k + 1
        while end < total and (blocks[total - end], blocks[total - 1 - end]) == shape:
            end += 1
        lax.fori_loop(k, end, lambda i, _: step(i, *shape), None)
        k = end


def blur_kernel(half, mine, other, weight, by, bz, out):
    planes, extent, ny = mine.shape
    parts = [(mine[x] + other[x]) * weight[x] for x in range(planes)]
    high, low = halves(jnp.concatenate(parts, axis=0))
    v = three(high, low, by[0], by[1])
    v = jnp.concatenate([v[x * extent:(x + 1) * extent] for x in range(planes)], axis=1)
    high, low = halves(v)
    block = 2 * half
    for b in range(out.shape[2] // block):
        rows = slice(b * block, b * block + 2 * block)
        w = dot(bz[0], high[rows]) + dot(bz[1], high[rows]) + dot(bz[0], low[rows])
        for x in range(planes):
            out[x, :, b * block:(b + 1) * block] = w[:, x * ny:(x + 1) * ny].T


def call(kernel, outs, in_spaces, scratch=(), flops=0):
    return pl.pallas_call(
        kernel,
        out_shape=outs,
        in_specs=[pl.BlockSpec(memory_space=space) for space in in_spaces],
        out_specs=jax.tree.map(lambda _: pl.BlockSpec(memory_space=VMEM), outs),
        scratch_shapes=list(scratch),
        compiler_params=pltpu.CompilerParams(vmem_limit_bytes=VMEM_BYTES),
        cost_estimate=pl.CostEstimate(flops=flops, bytes_accessed=1 << 20, transcendentals=0),
    )


def on_device(labels, classes, positions, phase_table, brightness, prop_taps, detect_taps):
    taps = prop_taps.shape[-1]
    plan = Plan(labels, positions.shape[0], taps)
    ny, half, block, cz = plan.ny, plan.half, plan.block, plan.cz
    f32, bf16 = jnp.float32, jnp.bfloat16
    tile, tiles = plan.tile, plan.tiles

    pieces = tile_pieces(plan, classes)
    far = [(swap(a, "sect", plan.cores), block_, ok) for a, block_, ok in pieces]

    def spread_over_cores(group, base):
        arrays, scalars = [], []
        for array, place, ok in group:
            for bits in range(plan.cores):
                arrays.append(array if bits == 0 else swap(array, "sect", bits))
                scalars += [base + (plan.core ^ bits) * plan.planes, place, ok]
        return arrays, scalars

    near_arrays, near_scalars = spread_over_cores(pieces, 0)
    far_arrays, far_scalars = spread_over_cores(far, plan.own)

    line = -(-max(4 * half, taps) // ny) * ny
    ky, kz, by, bz = call(
        functools.partial(prepare_kernel, ny, half),
        (
            jax.ShapeDtypeStruct((2, 2 * ny, 2 * ny), bf16),
            jax.ShapeDtypeStruct((2, 3, 2 * block, 2 * block), bf16),
            jax.ShapeDtypeStruct((2, ny, ny), bf16),
            jax.ShapeDtypeStruct((2, block, 2 * block), bf16),
        ),
        [VMEM] * 2,
        [pltpu.VMEM((8, line), f32)],
    )(prop_taps, detect_taps)

    table = jnp.stack([jnp.cos(phase_table), jnp.sin(phase_table)])
    size = 1 << (table.shape[1] - 1).bit_length()
    table = jnp.pad(table, [(0, 0), (0, size - table.shape[1])])
    spans = [plan.span(left) for left in range(plan.all_x + 1)]
    blocks = tuple(n for _, n in spans)
    width = plan.sheets * ny
    rows = plan.rows
    at = [plan.side, plan.home(), tile > 0, tile < tiles - 1, tile % 2, plan.core]

    def sweep(total, arrays, scalars, outs, *more):
        scal = at + scalars + [s for s, _ in spans[:total + 1]]
        scal = jnp.stack([jnp.asarray(s, jnp.int32) for s in scal])
        return call(
            functools.partial(beams_kernel, plan, blocks[:total + 1], len(arrays), total),
            outs,
            [SMEM] * 4 + [VMEM] * (2 + len(arrays) + len(more)),
            [
                pltpu.VMEM((total, rows, ny), f32),
                pltpu.VMEM((total, rows, ny), f32),
                pltpu.VMEM((2, rows + 2 * half, width), f32),
                pltpu.VMEM((2, rows + 2 * half, width), f32),
            ],
            flops=total * 6 * 10**8,
        )(scal, positions, table, brightness, ky, kz, *arrays, *more)

    even = tile % 2 == 0
    late, _ = lax.optimization_barrier((labels, pieces[-1][0]))
    first, last = late[..., :half], late[..., cz - half:]
    pairs = [(i, i ^ 1) for i in range(tiles) if i ^ 1 < tiles]
    gaps = [(i, ((i + 1) ^ 1) - 1) for i in range(1, tiles) if ((i + 1) ^ 1) - 1 < tiles]
    facing = lax.ppermute(jnp.where(even, last, first), "tile", pairs)
    beyond = lax.ppermute(jnp.where(even, first, last), "tile", gaps)

    sums = jax.ShapeDtypeStruct((plan.own, plan.extent, ny), f32)
    weights = jax.ShapeDtypeStruct((plan.planes, plan.extent, ny), f32)
    collected = sweep(plan.own, near_arrays, near_scalars, sums)
    collected, weight = sweep(
        2 * plan.own, near_arrays + far_arrays, near_scalars + far_scalars, (sums, weights),
        collected, labels, facing, beyond,
    )

    parts = collected.reshape(plan.cores, plan.planes, plan.extent, ny)
    mine = lax.dynamic_index_in_dim(parts, plan.core, 0, keepdims=False)
    other = jnp.zeros_like(mine)
    for bits in range(1, plan.cores):
        leaving = lax.dynamic_index_in_dim(parts, plan.core ^ bits, 0, keepdims=False)
        other = other + swap(leaving, "sect", bits) if bits > 1 else swap(leaving, "sect", bits)
    return call(
        functools.partial(blur_kernel, half),
        jax.ShapeDtypeStruct((plan.planes, ny, cz), f32),
        [VMEM] * 5,
    )(mine, other, weight, by, bz)


def solution(mesh):
    spread = P(("groups", "sect"), None, "tile")
    in_specs = (spread, spread, P("groups"), P(), P(), P(), P())
    return jax.shard_map(
        on_device, mesh=mesh, in_specs=in_specs, out_specs=spread, check_vma=False
    )
```

```python
import functools

import jax
import jax.numpy as jnp
from jax import lax
from jax.experimental import pallas as pl
from jax.experimental.pallas import tpu as pltpu
from jax.sharding import PartitionSpec as P

SHEET_WIDTH = 6.0
AMPLITUDE = 2.0
ROOM = 10 * 1024 * 1024
PIN = 1 << 40
SMEM = pltpu.SMEM
VMEM = pltpu.VMEM
HBM = pltpu.HBM


class Plan:
    def __init__(self, labels, positions, taps):
        self.planes, self.ny, self.cz = labels.shape
        self.half = taps // 2
        self.tiles = lax.axis_size("tile")
        self.cores = lax.axis_size("sect") // 2
        self.own = self.cores * self.planes
        self.all_x = 2 * self.own
        self.sheets = -(-positions // self.cores)
        self.block = 2 * self.half
        self.units = self.cz // self.half
        self.reach = -(-(self.all_x + 1) * self.half // self.cz)
        self.whole = self.tiles <= 2 * self.reach + 1
        self.window = self.tiles if self.whole else 2 * self.reach + 1
        self.rows = self.window * self.cz
        self.extent = self.cz + 2 * self.half
        self.width = self.sheets * self.ny

    def here(self):
        sect = lax.axis_index("sect")
        return lax.axis_index("tile"), sect // self.cores, lax.rem(sect, self.cores)

    def blocks(self, left):
        need = self.units + 2 + 2 * left
        return (min(need, self.window * self.units) if self.whole else need) // 2

    def start(self, left):
        if self.whole:
            last = jnp.maximum(self.window * self.units - (self.units + 2 + 2 * left), 0)
            unit = jnp.clip(lax.axis_index("tile") * self.units - 1 - left, 0, last)
        else:
            unit = self.reach * self.units - 1 - left
        return unit * self.half

    def home(self):
        return lax.axis_index("tile") * self.cz if self.whole else self.reach * self.cz


def swap(x, axis, bits):
    count = lax.axis_size(axis)
    return lax.ppermute(x, axis, [(i, i ^ bits) for i in range(count)])


def shift(x, axis, step):
    count = lax.axis_size(axis)
    return lax.ppermute(x, axis, [(i, i + step) for i in range(count) if 0 <= i + step < count])


def after(x, *done):
    return lax.optimization_barrier((x, *done))[0]


def tile_pieces(plan, mine, start, crossed):
    if plan.whole and plan.tiles & (plan.tiles - 1) == 0:
        got = {0: mine}
        if plan.tiles == 4:
            got[3] = swap(mine, "tile", 3)
            got[1] = swap(after(mine, *start), "tile", 1)
            got[2] = swap(after(got[3], *crossed), "tile", 1)
        else:
            for bits in range(1, plan.tiles):
                got[bits] = swap(mine, "tile", bits)
        return list(got.values()), [("xor", bits) for bits in got]
    if plan.whole:
        turns = range(plan.tiles)
        count = plan.tiles
        pieces = [
            lax.ppermute(mine, "tile", [(i, (i + k) % count) for i in range(count)]) if k else mine
            for k in turns
        ]
        return pieces, [("turn", k) for k in turns]
    steps = sorted(range(-plan.reach, plan.reach + 1), key=abs)
    return [shift(mine, "tile", -k) if k else mine for k in steps], [("step", k) for k in steps]


def block_of(plan, source):
    kind, k = source
    tile = lax.axis_index("tile")
    if kind == "xor":
        return tile ^ k, None
    if kind == "turn":
        return lax.rem(tile - k + plan.tiles, plan.tiles), None
    return k + plan.reach, (tile + k >= 0) & (tile + k < plan.tiles)


def halves(x):
    high = x.astype(jnp.bfloat16)
    return high, (x - high.astype(jnp.float32)).astype(jnp.bfloat16)


def dot(a, b):
    return jnp.dot(a, b, preferred_element_type=jnp.float32)


def three(high, low, matrix_high, matrix_low):
    return dot(high, matrix_high) + dot(low, matrix_high) + dot(high, matrix_low)


def circulant(row, size, half):
    wide = jnp.broadcast_to(row, (size, size))
    return pltpu.roll(wide, (size - half) % size, 1, stride=1, stride_axis=0).T


def band(row, size, wide):
    return pltpu.roll(jnp.broadcast_to(row, (size, wide)), 0, 1, stride=1, stride_axis=0)


def complex_matrix(diagonal, upper, lower):
    top = jnp.concatenate([diagonal, upper], axis=1)
    return jnp.concatenate([top, jnp.concatenate([lower, diagonal], axis=1)], axis=0)


def fetch(pairs, sems):
    copies = [pltpu.make_async_copy(src, dst, sems.at[i]) for i, (src, dst) in enumerate(pairs)]
    for copy in copies:
        copy.start()
    return copies


def build_bands(plan, taps, dtaps, phases, positions, ky, kz, by, bz, table, sheet, line):
    ny, half, block = plan.ny, plan.half, plan.block
    wide = 2 * block
    count = taps.shape[2]

    def padded(row):
        line[...] = jnp.zeros(line.shape, jnp.float32)
        line[0:1, :count] = row
        return line[0:1, :]

    def folded(row):
        spread = padded(row)
        return sum(spread[:, i:i + ny] for i in range(0, spread.shape[1], ny))

    def keep(ref, matrix, place=()):
        ref[(0, *place)], ref[(1, *place)] = halves(matrix)

    cyr = circulant(folded(taps[0, 0:1, :]), ny, half)
    cyi = circulant(folded(taps[0, 1:2, :]), ny, half)
    keep(ky, complex_matrix(cyr, cyi, -cyi))
    czr = band(padded(taps[1, 0:1, :])[:, :wide], block, wide)
    czi = band(padded(taps[1, 1:2, :])[:, :wide], block, wide)
    early = complex_matrix(czr[:, :block], -czi[:, :block], czi[:, :block])
    late = complex_matrix(czr[:, block:], -czi[:, block:], czi[:, block:])
    for number, matrix in enumerate((early, early + late, late)):
        keep(kz, matrix, (number,))
    keep(by, circulant(folded(dtaps[0:1, :]), ny, half))
    keep(bz, band(padded(dtaps[1:2, :])[:, :wide], block, wide))

    table[0:1, :] = jnp.cos(phases[...])
    table[1:2, :] = jnp.sin(phases[...])
    core = plan.here()[2]
    lane = lax.broadcasted_iota(jnp.int32, (1, ny), 1).astype(jnp.float32)
    for p in range(plan.sheets):
        number = core * plan.sheets + p
        live = number < positions.shape[0]
        centre = positions[jnp.where(live, number, 0)].astype(jnp.float32)
        offset = (lane - centre) / SHEET_WIDTH
        sheet[:, p * ny:(p + 1) * ny] = jnp.where(live, AMPLITUDE, 0.0) * jnp.exp(-offset * offset)


def choose(index, values):
    size = 1 << (len(values) - 1).bit_length()
    values = list(values) + [values[-1]] * (size - len(values))
    for b in range(size.bit_length() - 1):
        bit = (index & (1 << b)) != 0
        values = [jnp.where(bit, values[i + 1], values[i]) for i in range(0, len(values), 2)]
    return values[0]


def look_up(plan, sources, pieces, table, cosine, sine):
    cz = plan.cz
    core = plan.here()[2]
    entries = [[table[part:part + 1, e:e + 1] for e in range(table.shape[1])] for part in range(2)]
    for number, piece in pieces:
        block, valid = block_of(plan, sources[number // plan.cores])
        first = (core ^ (number % plan.cores)) * plan.planes
        row = pl.multiple_of(block * cz, cz)
        for plane in range(plan.planes):
            kind = piece[plane].T
            for values, target in zip(entries, (cosine, sine)):
                value = choose(kind, values)
                value = value if valid is None else jnp.where(valid, value, 0.0)
                target[first + plane, pl.ds(row, cz), :] = value


def enter(plan, sheet, field, spread):
    half, rows = plan.half, plan.rows
    wide = (rows, plan.width)
    field[0, half:half + rows, :] = jnp.broadcast_to(sheet[...], wide)
    field[1, half:half + rows, :] = jnp.zeros(wide, jnp.float32)
    for ref in (field, spread):
        for d in range(2):
            ref[d, :half, :] = jnp.zeros((half, plan.width), jnp.float32)
            ref[d, half + rows:, :] = jnp.zeros((half, plan.width), jnp.float32)


def propagate(plan, cos_at, sin_at, left, sources, targets, ky, kz, field, spread):
    ny, half, block, sheets = plan.ny, plan.half, plan.block, plan.sheets
    source, target = plan.start(left + 1), plan.start(left)

    def each(number, body):
        if plan.whole:
            for b in range(number):
                body(b)
        else:
            lax.fori_loop(0, number, lambda b, _: body(b), None)

    def turn(b):
        row = pl.multiple_of(source + b * block, half)
        cos, sin = cos_at(row, block), sin_at(row, block)
        parts = []
        for p in range(sheets):
            lanes = slice(p * ny, (p + 1) * ny)
            re = field[0, pl.ds(row + half, block), lanes]
            im = field[1, pl.ds(row + half, block), lanes]
            parts.append(jnp.concatenate([re * cos - im * sin, re * sin + im * cos], axis=1))
        high, low = halves(jnp.concatenate(parts, axis=0))
        v = three(high, low, ky[0], ky[1])
        for d in range(2):
            spread[d, pl.ds(row + half, block), :] = jnp.concatenate(
                [v[p * block:(p + 1) * block, d * ny:(d + 1) * ny] for p in range(sheets)], axis=1
            )

    def product(number, x):
        high, low = halves(x)
        return dot(kz[0, number], high) + dot(kz[1, number], high) + dot(kz[0, number], low)

    def window(row):
        return jnp.concatenate([spread[d, pl.ds(row, block), :] for d in range(2)], axis=0)

    def store(row, w):
        field[0, pl.ds(row + half, block), :] = w[:block]
        field[1, pl.ds(row + half, block), :] = w[block:]

    def pair(b):
        row = pl.multiple_of(target + 2 * b * block, half)
        x = [window(row + i * block) for i in range(3)]
        middle = product(1, x[1])
        store(row, product(0, x[0] - x[1]) + middle)
        store(row + block, product(2, x[2] - x[1]) + middle)

    def single(b):
        row = pl.multiple_of(target + b * block, half)
        store(row, product(0, window(row)) + product(2, window(row + block)))

    each(sources, turn)
    each(targets // 2, pair)
    if targets % 2:
        single(targets - 1)


def energy(plan, field):
    home = pl.multiple_of(plan.home(), plan.half)
    re = field[0, pl.ds(home, plan.extent), :]
    im = field[1, pl.ds(home, plan.extent), :]
    every = re * re + im * im
    total = every[:, :plan.ny]
    for p in range(1, plan.sheets):
        total = total + every[:, p * plan.ny:(p + 1) * plan.ny]
    return total


def steps_of(plan, begin, end, step, total):
    def shape(k):
        return plan.blocks(total - k), plan.blocks(total - 1 - k)

    k = begin
    while k < end:
        last = k + 1
        while last < end and shape(last) == shape(k):
            last += 1
        lax.fori_loop(k, last, lambda i, _, s=shape(k): step(i, *s), None)
        k = last


def short_kernel(plan, sources, hbm_taps, hbm_dtaps, hbm_phases, hbm_positions, hbm_mine, *refs):
    count = len(sources) * plan.cores - 1
    pieces = refs[:count]
    out, ky, kz, by, bz, table, sheet, hbm_cosine, hbm_sine = refs[count:count + 9]
    taps, dtaps, phases, positions, mine, cosine, sine, field, spread, line, sems = refs[count + 9:]
    pairs = [(hbm_phases, phases), (hbm_positions, positions), (hbm_taps, taps), (hbm_dtaps, dtaps)]
    *small, arriving = fetch([*pairs, (hbm_mine, mine)], sems)
    for copy in small:
        copy.wait()
    build_bands(plan, taps, dtaps, phases, positions, ky, kz, by, bz, table, sheet, line)
    own = plan.own
    enter(plan, sheet, field, spread)
    look_up(plan, sources, list(enumerate(pieces, 1)), table, cosine, sine)
    arriving.wait()
    look_up(plan, sources, [(0, mine)], table, cosine, sine)
    leaving = fetch([(cosine, hbm_cosine), (sine, hbm_sine)], sems)
    side = plan.here()[1]

    def step(k, reads, writes):
        slot = jnp.where(side == 0, k, own - 1 - k)
        maps = [lambda row, n, ref=ref: ref[slot, pl.ds(row, n), :] for ref in (cosine, sine)]
        propagate(plan, *maps, own - 1 - k, reads, writes, ky, kz, field, spread)
        out[slot] = energy(plan, field)

    steps_of(plan, 0, own, step, own)
    for copy in leaving:
        copy.wait()


def long_kernel(plan, sources, ky, kz, table, sheet, hbm_cosine, hbm_sine, earlier, *refs):
    count = len(sources) * plan.cores
    pieces = refs[:count]
    out, far_cosine, far_sine, cosine, sine, field, spread, sems = refs[count:]
    own = plan.own
    arriving = fetch([(hbm_cosine, cosine), (hbm_sine, sine)], sems)
    enter(plan, sheet, field, spread)
    look_up(plan, sources, list(enumerate(pieces)), table, far_cosine, far_sine)
    side = plan.here()[1]

    def far_step(k, reads, writes):
        slot = jnp.where(side == 0, own - 1 - k, k)
        maps = [lambda row, n, ref=ref: ref[slot, pl.ds(row, n), :] for ref in (far_cosine, far_sine)]
        propagate(plan, *maps, 2 * own - 1 - k, reads, writes, ky, kz, field, spread)

    def step(k, reads, writes):
        slot = jnp.where(side == 0, 2 * own - 1 - k, k - own)
        maps = [lambda row, n, ref=ref: ref[slot, pl.ds(row, n), :] for ref in (cosine, sine)]
        propagate(plan, *maps, 2 * own - 1 - k, reads, writes, ky, kz, field, spread)
        out[slot] = earlier[slot] + energy(plan, field)

    steps_of(plan, 0, own, far_step, 2 * own)
    for copy in arriving:
        copy.wait()
    steps_of(plan, own, 2 * own, step, 2 * own)


def blur_kernel(plan, mine, other, hbm_bright, hbm_labels, facing, beyond, by, bz, out, bright, labels, sems):
    half, ny, extent = plan.half, plan.ny, plan.extent
    first, arriving = fetch([(hbm_bright, bright), (hbm_labels, labels)], sems)
    first.wait()
    tile = lax.axis_index("tile")
    even = lax.rem(tile, 2) == 0
    first_half = lax.broadcasted_iota(jnp.int32, (ny, 2 * half), 1) < half
    ends = [(tile < plan.tiles - 1).astype(jnp.float32), (tile > 0).astype(jnp.float32)]
    inside = jnp.where(first_half, ends[0], ends[1])
    values = [bright[e] for e in range(bright.shape[0])]
    halos = []
    for x in range(plan.planes):
        before = jnp.where(even, beyond[x], facing[x])[:, -2 * half:]
        behind = jnp.where(even, facing[x], beyond[x])[:, :2 * half]
        halos.append((choose(jnp.where(first_half, behind, before), values) * inside).T)
    arriving.wait()
    parts = []
    for x in range(plan.planes):
        weight = jnp.concatenate([halos[x][half:], choose(labels[x], values).T, halos[x][:half]], axis=0)
        parts.append((mine[x] + other[x]) * weight)
    high, low = halves(jnp.concatenate(parts, axis=0))
    v = three(high, low, by[0], by[1])
    v = jnp.concatenate([v[x * extent:(x + 1) * extent] for x in range(plan.planes)], axis=1)
    high, low = halves(v)
    block = plan.block
    for b in range(plan.cz // block):
        rows = slice(b * block, b * block + 2 * block)
        w = dot(bz[0], high[rows]) + dot(bz[1], high[rows]) + dot(bz[0], low[rows])
        for x in range(plan.planes):
            out[x, :, b * block:(b + 1) * block] = w[:, x * ny:(x + 1) * ny].T


def size_of(x):
    return x.size * x.dtype.itemsize


def call(kernel, outs, in_spaces, scratch=(), flops=0, out_spaces=None):
    return lambda *args: call_with(args, kernel, outs, in_spaces, scratch, flops, out_spaces)


def call_with(args, kernel, outs, in_spaces, scratch, flops, out_spaces):
    args = [
        pltpu.with_memory_space_constraint(x, space) if space is HBM or size_of(x) > PIN else x
        for x, space in zip(args, in_spaces)
    ]
    held = [x for x, space in zip(args, in_spaces) if space is VMEM]
    held += jax.tree.leaves(outs)
    held += [jax.ShapeDtypeStruct(x.shape, x.dtype) for x in scratch if x.memory_space == VMEM]
    if out_spaces is None:
        out_spaces = jax.tree.map(lambda _: VMEM, outs)
    limit = ROOM + sum(size_of(x) for x in held)
    flat, tree = jax.tree.flatten(outs)
    spaces = jax.tree.leaves(out_spaces)
    outs = tree.unflatten(
        [HBM(x.shape, x.dtype) if space is HBM else x for x, space in zip(flat, spaces)]
    )
    return pl.pallas_call(
        kernel,
        out_shape=outs,
        in_specs=[pl.BlockSpec(memory_space=space) for space in in_spaces],
        out_specs=jax.tree.map(lambda space: pl.BlockSpec(memory_space=space), out_spaces),
        scratch_shapes=list(scratch),
        compiler_params=pltpu.CompilerParams(vmem_limit_bytes=limit),
        cost_estimate=pl.CostEstimate(flops=flops, bytes_accessed=1 << 20, transcendentals=0),
    )(*args)


def on_device(labels, classes, positions, phase_table, brightness, prop_taps, detect_taps):
    taps = prop_taps.shape[-1]
    plan = Plan(labels, positions.shape[0], taps)
    ny, half, block, rows = plan.ny, plan.half, plan.block, plan.rows
    tiles, cores = plan.tiles, plan.cores
    core = plan.here()[2]
    f32, bf16 = jnp.float32, jnp.bfloat16
    shape = jax.ShapeDtypeStruct

    def over_cores(array):
        return [array] + [swap(array, "sect", bits) for bits in range(1, cores)]

    crossed = [swap(classes, "sect", cores)]
    pieces, sources = tile_pieces(plan, classes, (), crossed)
    near = []
    for number, piece in enumerate(pieces):
        shared = over_cores(piece)
        near += shared
        if number:
            hold = number < len(pieces) - 1
            crossed.append(swap(after(piece, *shared[1:]) if hold else piece, "sect", cores))

    maps = shape((plan.own, rows, ny), f32)
    whole_maps = pltpu.VMEM((plan.own, rows, ny), f32)
    state = pltpu.VMEM((2, rows + 2 * half, plan.width), f32)
    sums = shape((plan.own, plan.extent, ny), f32)
    line = -(-max(4 * half, taps) // ny) * ny
    phases = phase_table[None]
    near[1] = after(near[1], crossed[len(crossed) // 2])
    sums, ky, kz, by, bz, table, sheet, cosine, sine = call(
        functools.partial(short_kernel, plan, sources),
        (
            sums,
            shape((2, 2 * ny, 2 * ny), bf16),
            shape((2, 3, 2 * block, 2 * block), bf16),
            shape((2, ny, ny), bf16),
            shape((2, block, 2 * block), bf16),
            shape((2, phases.shape[1]), f32),
            shape((1, plan.width), f32),
            maps,
            maps,
        ),
        [HBM] * 5 + [VMEM] * (len(near) - 1),
        [
            pltpu.VMEM(prop_taps.shape, f32),
            pltpu.VMEM(detect_taps.shape, f32),
            pltpu.VMEM(phases.shape, f32),
            pltpu.SMEM(positions.shape, positions.dtype),
            pltpu.VMEM(classes.shape, classes.dtype),
            whole_maps,
            whole_maps,
            state,
            state,
            pltpu.VMEM((8, line), f32),
            pltpu.SemaphoreType.DMA((5,)),
        ],
        flops=3 * 10**9,
        out_spaces=(VMEM,) * 7 + (HBM,) * 2,
    )(prop_taps, detect_taps, phases, positions, *near)

    pairs = [(i, i ^ 1) for i in range(tiles) if i ^ 1 < tiles]
    gaps = [(i, ((i + 1) ^ 1) - 1) for i in range(1, tiles) if ((i + 1) ^ 1) - 1 < tiles]
    if tiles == 4:
        gaps = [(i, i ^ 3) for i in range(tiles)]
    late = after(labels, sums)
    facing = lax.ppermute(late, "tile", pairs)
    beyond = lax.ppermute(late, "tile", gaps)

    far = []
    for number, piece in enumerate(crossed):
        last = number == len(crossed) - 1
        far += [piece] + over_cores(after(piece, sums) if last else piece)[1:]
    sums = call(
        functools.partial(long_kernel, plan, sources),
        shape((plan.own, plan.extent, ny), f32),
        [VMEM] * 4 + [HBM] * 2 + [VMEM] * (1 + len(far)),
        [whole_maps] * 4 + [state, state, pltpu.SemaphoreType.DMA((2,))],
        flops=6 * 10**9,
    )(ky, kz, table, sheet, cosine, sine, sums, *far)

    parts = sums.reshape(cores, plan.planes, plan.extent, ny)
    mine = lax.dynamic_index_in_dim(parts, core, 0, keepdims=False)
    other = None
    for bits in range(1, cores):
        leaving = lax.dynamic_index_in_dim(parts, core ^ bits, 0, keepdims=False)
        arrived = swap(after(leaving, facing, beyond), "sect", bits)
        other = arrived if other is None else other + arrived
    other = jnp.zeros_like(mine) if other is None else other
    return call(
        functools.partial(blur_kernel, plan),
        shape((plan.planes, ny, plan.cz), f32),
        [VMEM] * 2 + [HBM] * 2 + [VMEM] * 4,
        [
            pltpu.SMEM(brightness.shape, f32),
            pltpu.VMEM(labels.shape, labels.dtype),
            pltpu.SemaphoreType.DMA((2,)),
        ],
    )(mine, other, brightness, labels, facing, beyond, by, bz)


def solution(mesh):
    spread = P(("groups", "sect"), None, "tile")
    in_specs = (spread, spread, P("groups"), P(), P(), P(), P())
    return jax.shard_map(
        on_device, mesh=mesh, in_specs=in_specs, out_specs=spread, check_vma=False
    )
```

```python
import functools
import operator

import jax
import jax.numpy as jnp
from jax import lax
from jax.experimental import pallas as pl
from jax.experimental.pallas import tpu as pltpu
from jax.sharding import PartitionSpec as P

SHEET_WIDTH = 6.0
AMPLITUDE = 2.0
ROOM = 10 * 1024 * 1024
PIN = 1 << 40
SMEM = pltpu.SMEM
VMEM = pltpu.VMEM
HBM = pltpu.HBM


class Plan:
    def __init__(self, labels, positions, taps):
        self.planes, self.ny, self.cz = labels.shape
        self.half = taps // 2
        self.tiles = lax.axis_size("tile")
        self.cores = lax.axis_size("sect") // 2
        self.own = self.cores * self.planes
        self.all_x = 2 * self.own
        self.sheets = -(-positions // self.cores)
        self.block = 2 * self.half
        self.units = self.cz // self.half
        self.reach = -(-(self.all_x + 1) * self.half // self.cz)
        self.whole = self.tiles <= 2 * self.reach + 1
        self.window = self.tiles if self.whole else 2 * self.reach + 1
        self.rows = self.window * self.cz
        self.extent = self.cz + 2 * self.half
        self.width = self.sheets * self.ny

    def here(self):
        sect = lax.axis_index("sect")
        return lax.axis_index("tile"), sect // self.cores, lax.rem(sect, self.cores)

    def blocks(self, left):
        need = self.units + 2 + 2 * left
        return (min(need, self.window * self.units) if self.whole else need) // 2

    def start(self, left):
        left = operator.index(left)
        if self.whole:
            last = max(self.window * self.units - (self.units + 2 + 2 * left), 0)
            unit = 0 if last == 0 else jnp.clip(lax.axis_index("tile") * self.units - 1 - left, 0, last)
        else:
            unit = self.reach * self.units - 1 - left
        return unit * self.half

    def home(self):
        return lax.axis_index("tile") * self.cz if self.whole else self.reach * self.cz


def swap(x, axis, bits):
    count = lax.axis_size(axis)
    return lax.ppermute(x, axis, [(i, i ^ bits) for i in range(count)])


def shift(x, axis, step):
    count = lax.axis_size(axis)
    return lax.ppermute(x, axis, [(i, i + step) for i in range(count) if 0 <= i + step < count])


def after(x, *done):
    return lax.optimization_barrier((x, *done))[0]


def tile_pieces(plan, mine, crossed):
    if plan.whole and plan.tiles & (plan.tiles - 1) == 0:
        got = {0: mine}
        if plan.tiles == 4:
            got[3] = swap(mine, "tile", 3)
            got[1] = swap(mine, "tile", 1)
            got[2] = swap(after(got[3], *crossed), "tile", 1)
        else:
            for bits in range(1, plan.tiles):
                got[bits] = swap(mine, "tile", bits)
        return list(got.values()), [("xor", bits) for bits in got]
    if plan.whole:
        turns = range(plan.tiles)
        count = plan.tiles
        pieces = [
            lax.ppermute(mine, "tile", [(i, (i + k) % count) for i in range(count)]) if k else mine
            for k in turns
        ]
        return pieces, [("turn", k) for k in turns]
    steps = sorted(range(-plan.reach, plan.reach + 1), key=abs)
    return [shift(mine, "tile", -k) if k else mine for k in steps], [("step", k) for k in steps]


def block_of(plan, source):
    kind, k = source
    tile = lax.axis_index("tile")
    if kind == "xor":
        return tile ^ k, None
    if kind == "turn":
        return lax.rem(tile - k + plan.tiles, plan.tiles), None
    return k + plan.reach, (tile + k >= 0) & (tile + k < plan.tiles)


def aligned(row, size):
    return row if isinstance(row, int) else pl.multiple_of(row, size)


def halves(x):
    high = x.astype(jnp.bfloat16)
    return high, (x - high.astype(jnp.float32)).astype(jnp.bfloat16)


def dot(a, b):
    return jnp.dot(a, b, preferred_element_type=jnp.float32)


def three(high, low, matrix_high, matrix_low):
    return dot(high, matrix_high) + dot(low, matrix_high) + dot(high, matrix_low)


def circulant(row, size, half):
    wide = jnp.broadcast_to(row, (size, size))
    return pltpu.roll(wide, (size - half) % size, 1, stride=1, stride_axis=0).T


def band(row, size, wide):
    return pltpu.roll(jnp.broadcast_to(row, (size, wide)), 0, 1, stride=1, stride_axis=0)


def complex_matrix(diagonal, upper, lower):
    top = jnp.concatenate([diagonal, upper], axis=1)
    return jnp.concatenate([top, jnp.concatenate([lower, diagonal], axis=1)], axis=0)


def fetch(pairs, sems):
    copies = [pltpu.make_async_copy(src, dst, sems.at[i]) for i, (src, dst) in enumerate(pairs)]
    for copy in copies:
        copy.start()
    return copies


def prepare_kernel(plan, count, hbm_taps, hbm_dtaps, hbm_phases, hbm_positions, *refs):
    joined, refs = refs[:count], refs[count:]
    ky, kz, km, by, bz, table, sheet, together, taps, dtaps, phases, positions, line, sems = refs
    ny, half, block = plan.ny, plan.half, plan.block
    wide = 2 * block
    count = taps.shape[2]
    pairs = [(hbm_taps, taps), (hbm_dtaps, dtaps), (hbm_phases, phases), (hbm_positions, positions)]
    copies = fetch(pairs, sems)
    for number, piece in enumerate(joined):
        together[number * plan.planes:(number + 1) * plan.planes] = piece[...]
    for copy in copies:
        copy.wait()

    def padded(row):
        line[...] = jnp.zeros(line.shape, jnp.float32)
        line[0:1, :count] = row
        return line[0:1, :]

    def folded(row):
        spread = padded(row)
        return sum(spread[:, i:i + ny] for i in range(0, spread.shape[1], ny))

    def keep(ref, matrix, place=()):
        ref[(0, *place)], ref[(1, *place)] = halves(matrix)

    cyr = circulant(folded(taps[0, 0:1, :]), ny, half)
    cyi = circulant(folded(taps[0, 1:2, :]), ny, half)
    keep(ky, complex_matrix(cyr, cyi, -cyi))
    czr = band(padded(taps[1, 0:1, :])[:, :wide], block, wide)
    czi = band(padded(taps[1, 1:2, :])[:, :wide], block, wide)
    early = complex_matrix(czr[:, :block], -czi[:, :block], czi[:, :block])
    late = complex_matrix(czr[:, block:], -czi[:, block:], czi[:, block:])
    keep(kz, early, (0,))
    keep(kz, late, (1,))
    middle = early + late
    quarter = [
        [[middle[d:d + half, c + e:c + e + half] for c in (0, block)] for d in (0, block)] for e in (0, half)
    ]
    for number, sign in enumerate((1.0, -1.0)):
        part = jnp.concatenate(
            [jnp.concatenate([quarter[0][d][c] + sign * quarter[1][d][c] for c in range(2)], axis=1) for d in range(2)],
            axis=0,
        )
        high, low = halves(0.5 * part)
        km[number] = jnp.concatenate(
            [jnp.concatenate([high, high], axis=1), jnp.concatenate([low, low], axis=1)], axis=0
        )
    keep(by, circulant(folded(dtaps[0:1, :]), ny, half))
    keep(bz, band(padded(dtaps[1:2, :])[:, :wide], block, wide))

    table[0:1, :] = jnp.cos(phases[...])
    table[1:2, :] = jnp.sin(phases[...])
    core = plan.here()[2]
    lane = lax.broadcasted_iota(jnp.int32, (1, ny), 1).astype(jnp.float32)
    for p in range(plan.sheets):
        number = core * plan.sheets + p
        live = number < positions.shape[0]
        centre = positions[jnp.where(live, number, 0)].astype(jnp.float32)
        offset = (lane - centre) / SHEET_WIDTH
        sheet[:, p * ny:(p + 1) * ny] = jnp.where(live, AMPLITUDE, 0.0) * jnp.exp(-offset * offset)


def choose(index, values):
    size = 1 << (len(values) - 1).bit_length()
    values = list(values) + [values[-1]] * (size - len(values))
    for b in range(size.bit_length() - 1):
        bit = (index & (1 << b)) != 0
        values = [jnp.where(bit, values[i + 1], values[i]) for i in range(0, len(values), 2)]
    return values[0]


def look_up(plan, groups, pieces, table, cosine, sine):
    cz = plan.cz
    core = plan.here()[2]
    entries = [[table[part:part + 1, e:e + 1] for e in range(table.shape[1])] for part in range(2)]
    for number, piece in pieces:
        first = (core ^ (number % plan.cores)) * plan.planes
        for place, source in enumerate(groups[number // plan.cores]):
            block, valid = block_of(plan, source)
            row = pl.multiple_of(block * cz, cz)
            for plane in range(plan.planes):
                kind = piece[place * plan.planes + plane].T
                for values, target in zip(entries, (cosine, sine)):
                    value = choose(kind, values)
                    value = value if valid is None else jnp.where(valid, value, 0.0)
                    target[first + plane, pl.ds(row, cz), :] = value


def enter(plan, sheet, field, spread):
    half, rows = plan.half, plan.rows
    wide = (rows, plan.width)
    field[0, half:half + rows, :] = jnp.broadcast_to(sheet[...], wide)
    field[1, half:half + rows, :] = jnp.zeros(wide, jnp.float32)
    for ref in (field, spread):
        for d in range(2):
            ref[d, :half, :] = jnp.zeros((half, plan.width), jnp.float32)
            ref[d, half + rows:, :] = jnp.zeros((half, plan.width), jnp.float32)


def propagate(plan, cos_at, sin_at, left, ky, kz, km, field, spread):
    ny, half, block, sheets = plan.ny, plan.half, plan.block, plan.sheets
    source, target = plan.start(left + 1), plan.start(left)
    sources, targets = plan.blocks(left + 1), plan.blocks(left)

    def each(number, body):
        if plan.whole:
            for b in range(number):
                body(b)
        else:
            lax.fori_loop(0, number, lambda b, _: body(b), None)

    def turn(b):
        row = aligned(source + b * block, half)
        cos, sin = cos_at(row, block), sin_at(row, block)
        parts = []
        for p in range(sheets):
            lanes = slice(p * ny, (p + 1) * ny)
            re = field[0, pl.ds(row + half, block), lanes]
            im = field[1, pl.ds(row + half, block), lanes]
            parts.append(jnp.concatenate([re * cos - im * sin, re * sin + im * cos], axis=1))
        high, low = halves(jnp.concatenate(parts, axis=0))
        v = three(high, low, ky[0], ky[1])
        for d in range(2):
            spread[d, pl.ds(row + half, block), :] = jnp.concatenate(
                [v[p * block:(p + 1) * block, d * ny:(d + 1) * ny] for p in range(sheets)], axis=1
            )

    def product(number, x):
        high, low = halves(x)
        return dot(kz[0, number], high) + dot(kz[1, number], high) + dot(kz[0, number], low)

    def circular(x):
        top = jnp.concatenate([x[:half], x[block:block + half]], axis=0)
        bottom = jnp.concatenate([x[half:block], x[block + half:]], axis=0)
        sides = []
        for number, part in enumerate((top + bottom, top - bottom)):
            w = dot(km[number], jnp.concatenate(halves(part), axis=0))
            sides.append(w[:block] + w[block:])
        top, bottom = sides[0] + sides[1], sides[0] - sides[1]
        return jnp.concatenate([top[:half], bottom[:half], top[half:], bottom[half:]], axis=0)

    def window(row):
        return jnp.concatenate([spread[d, pl.ds(row, block), :] for d in range(2)], axis=0)

    def store(row, w):
        field[0, pl.ds(row + half, block), :] = w[:block]
        field[1, pl.ds(row + half, block), :] = w[block:]

    def pair(b):
        row = aligned(target + 2 * b * block, half)
        x = [window(row + i * block) for i in range(3)]
        shared = circular(x[1])
        store(row, product(0, x[0] - x[1]) + shared)
        store(row + block, product(1, x[2] - x[1]) + shared)

    def single(b):
        row = aligned(target + b * block, half)
        store(row, product(0, window(row)) + product(1, window(row + block)))

    each(sources, turn)
    each(targets // 2, pair)
    if targets % 2:
        single(targets - 1)


def energy(plan, field):
    home = pl.multiple_of(plan.home(), plan.half)
    re = field[0, pl.ds(home, plan.extent), :]
    im = field[1, pl.ds(home, plan.extent), :]
    every = re * re + im * im
    total = every[:, :plan.ny]
    for p in range(1, plan.sheets):
        total = total + every[:, p * plan.ny:(p + 1) * plan.ny]
    return total


def short_kernel(plan, groups, hbm_mine, ky, kz, km, table, sheet, *refs):
    count = len(groups) * plan.cores - 1
    pieces = refs[:count]
    out, hbm_cosine, hbm_sine, mine, cosine, sine, field, spread, sems = refs[count:]
    own = plan.own
    (arriving,) = fetch([(hbm_mine, mine)], sems)
    enter(plan, sheet, field, spread)
    look_up(plan, groups, list(enumerate(pieces, 1)), table, cosine, sine)
    arriving.wait()
    look_up(plan, groups, [(0, mine)], table, cosine, sine)
    leaving = fetch([(cosine, hbm_cosine), (sine, hbm_sine)], sems)
    side = plan.here()[1]

    def step(k, left):
        slot = jnp.where(side == 0, k, own - 1 - k)
        maps = [lambda row, n, ref=ref: ref[slot, pl.ds(row, n), :] for ref in (cosine, sine)]
        propagate(plan, *maps, left, ky, kz, km, field, spread)
        out[slot] = energy(plan, field)

    for k in range(own):
        step(k, own - 1 - k)
    for copy in leaving:
        copy.wait()


def long_kernel(plan, groups, ky, kz, km, table, sheet, hbm_cosine, hbm_sine, earlier, *refs):
    count = len(groups) * plan.cores
    pieces = refs[:count]
    out, far_cosine, far_sine, cosine, sine, field, spread, sems = refs[count:]
    own = plan.own
    arriving = fetch([(hbm_cosine, cosine), (hbm_sine, sine)], sems)
    enter(plan, sheet, field, spread)
    look_up(plan, groups, list(enumerate(pieces)), table, far_cosine, far_sine)
    side = plan.here()[1]

    def far_step(k, left):
        slot = jnp.where(side == 0, own - 1 - k, k)
        maps = [lambda row, n, ref=ref: ref[slot, pl.ds(row, n), :] for ref in (far_cosine, far_sine)]
        propagate(plan, *maps, left, ky, kz, km, field, spread)

    def step(k, left):
        slot = jnp.where(side == 0, 2 * own - 1 - k, k - own)
        maps = [lambda row, n, ref=ref: ref[slot, pl.ds(row, n), :] for ref in (cosine, sine)]
        propagate(plan, *maps, left, ky, kz, km, field, spread)
        out[slot] = earlier[slot] + energy(plan, field)

    for k in range(own):
        far_step(k, 2 * own - 1 - k)
    for copy in arriving:
        copy.wait()
    for k in range(own, 2 * own):
        step(k, 2 * own - 1 - k)


def weight_kernel(plan, hbm_bright, hbm_labels, facing, beyond, weight, bright, labels, sems):
    half, ny, cz = plan.half, plan.ny, plan.cz
    first, arriving = fetch([(hbm_bright, bright), (hbm_labels, labels)], sems)
    first.wait()
    tile = lax.axis_index("tile")
    even = lax.rem(tile, 2) == 0
    first_half = lax.broadcasted_iota(jnp.int32, (ny, 2 * half), 1) < half
    ends = [(tile < plan.tiles - 1).astype(jnp.float32), (tile > 0).astype(jnp.float32)]
    inside = jnp.where(first_half, ends[0], ends[1])
    values = [bright[e] for e in range(bright.shape[0])]
    for x in range(plan.planes):
        before = jnp.where(even, beyond[x], facing[x])[:, -2 * half:]
        behind = jnp.where(even, facing[x], beyond[x])[:, :2 * half]
        halo = (choose(jnp.where(first_half, behind, before), values) * inside).T
        weight[x, :half, :] = halo[half:]
        weight[x, half + cz:, :] = halo[:half]
    arriving.wait()
    for x in range(plan.planes):
        weight[x, half:half + cz, :] = choose(labels[x], values).T


def blur_kernel(plan, mine, other, weight, by, bz, out):
    ny, extent, block = plan.ny, plan.extent, plan.block
    parts = [(mine[x] + other[x]) * weight[x] for x in range(plan.planes)]
    high, low = halves(jnp.concatenate(parts, axis=0))
    v = three(high, low, by[0], by[1])
    v = jnp.concatenate([v[x * extent:(x + 1) * extent] for x in range(plan.planes)], axis=1)
    high, low = halves(v)
    for b in range(plan.cz // block):
        rows = slice(b * block, b * block + 2 * block)
        w = dot(bz[0], high[rows]) + dot(bz[1], high[rows]) + dot(bz[0], low[rows])
        for x in range(plan.planes):
            out[x, :, b * block:(b + 1) * block] = w[:, x * ny:(x + 1) * ny].T


def size_of(x):
    return x.size * x.dtype.itemsize


def call(kernel, outs, in_spaces, scratch=(), flops=0, out_spaces=None):
    return lambda *args: call_with(args, kernel, outs, in_spaces, scratch, flops, out_spaces)


def call_with(args, kernel, outs, in_spaces, scratch, flops, out_spaces):
    args = [
        pltpu.with_memory_space_constraint(x, space) if space is HBM or size_of(x) > PIN else x
        for x, space in zip(args, in_spaces)
    ]
    held = [x for x, space in zip(args, in_spaces) if space is VMEM]
    held += jax.tree.leaves(outs)
    held += [jax.ShapeDtypeStruct(x.shape, x.dtype) for x in scratch if x.memory_space == VMEM]
    if out_spaces is None:
        out_spaces = jax.tree.map(lambda _: VMEM, outs)
    limit = ROOM + sum(size_of(x) for x in held)
    flat, tree = jax.tree.flatten(outs)
    spaces = jax.tree.leaves(out_spaces)
    outs = tree.unflatten(
        [HBM(x.shape, x.dtype) if space is HBM else x for x, space in zip(flat, spaces)]
    )
    return pl.pallas_call(
        kernel,
        out_shape=outs,
        in_specs=[pl.BlockSpec(memory_space=space) for space in in_spaces],
        out_specs=jax.tree.map(lambda space: pl.BlockSpec(memory_space=space), out_spaces),
        scratch_shapes=list(scratch),
        compiler_params=pltpu.CompilerParams(vmem_limit_bytes=limit),
        cost_estimate=pl.CostEstimate(flops=flops, bytes_accessed=1 << 20, transcendentals=0),
    )(*args)


def on_device(labels, classes, positions, phase_table, brightness, prop_taps, detect_taps):
    taps = prop_taps.shape[-1]
    plan = Plan(labels, positions.shape[0], taps)
    ny, half, block, rows = plan.ny, plan.half, plan.block, plan.rows
    tiles, cores = plan.tiles, plan.cores
    core = plan.here()[2]
    f32, bf16 = jnp.float32, jnp.bfloat16
    shape = jax.ShapeDtypeStruct

    def over_cores(array):
        return [array] + [swap(array, "sect", bits) for bits in range(1, cores)]

    crossed = [swap(classes, "sect", cores)]
    pieces, sources = tile_pieces(plan, classes, crossed)
    joined = pieces[1:-1]
    groups = (sources[:1], sources[1:-1], sources[-1:])
    line = -(-max(4 * half, taps) // ny) * ny
    phases = phase_table[None]
    ky, kz, km, by, bz, table, sheet, together = call(
        functools.partial(prepare_kernel, plan, len(joined)),
        (
            shape((2, 2 * ny, 2 * ny), bf16),
            shape((2, 2, 2 * block, 2 * block), bf16),
            shape((2, 2 * block, 2 * block), bf16),
            shape((2, ny, ny), bf16),
            shape((2, block, 2 * block), bf16),
            shape((2, phases.shape[1]), f32),
            shape((1, plan.width), f32),
            shape((len(joined) * plan.planes, ny, plan.cz), classes.dtype),
        ),
        [HBM] * 4 + [VMEM] * len(joined),
        [
            pltpu.VMEM(prop_taps.shape, f32),
            pltpu.VMEM(detect_taps.shape, f32),
            pltpu.VMEM(phases.shape, f32),
            pltpu.SMEM(positions.shape, positions.dtype),
            pltpu.VMEM((8, line), f32),
            pltpu.SemaphoreType.DMA((4,)),
        ],
    )(prop_taps, detect_taps, phases, positions, *joined)
    near = []
    for number, piece in enumerate((classes, together, pieces[-1])):
        near += over_cores(piece)
        if number:
            crossed.append(swap(piece, "sect", cores))

    maps = shape((plan.own, rows, ny), f32)
    whole_maps = pltpu.VMEM((plan.own, rows, ny), f32)
    state = pltpu.VMEM((2, rows + 2 * half, plan.width), f32)
    sums = shape((plan.own, plan.extent, ny), f32)
    sums, cosine, sine = call(
        functools.partial(short_kernel, plan, groups),
        (sums, maps, maps),
        [HBM] + [VMEM] * (4 + len(near)),
        [
            pltpu.VMEM(classes.shape, classes.dtype),
            whole_maps,
            whole_maps,
            state,
            state,
            pltpu.SemaphoreType.DMA((2,)),
        ],
        flops=3 * 10**9,
        out_spaces=(VMEM, HBM, HBM),
    )(near[0], ky, kz, km, table, sheet, *near[1:])

    pairs = [(i, i ^ 1) for i in range(tiles) if i ^ 1 < tiles]
    gaps = [(i, ((i + 1) ^ 1) - 1) for i in range(1, tiles) if ((i + 1) ^ 1) - 1 < tiles]
    if tiles == 4:
        gaps = [(i, i ^ 3) for i in range(tiles)]
    late = after(labels, sums)
    facing = lax.ppermute(late, "tile", pairs)
    beyond = lax.ppermute(late, "tile", gaps)

    far = []
    for piece in crossed:
        far += [piece] + over_cores(after(piece, sums))[1:]
    sums = call(
        functools.partial(long_kernel, plan, groups),
        shape((plan.own, plan.extent, ny), f32),
        [VMEM] * 5 + [HBM] * 2 + [VMEM] * (1 + len(far)),
        [whole_maps] * 4 + [state, state, pltpu.SemaphoreType.DMA((2,))],
        flops=6 * 10**9,
    )(ky, kz, km, table, sheet, cosine, sine, sums, *far)

    parts = sums.reshape(cores, plan.planes, plan.extent, ny)
    mine = lax.dynamic_index_in_dim(parts, core, 0, keepdims=False)
    other = None
    for bits in range(1, cores):
        leaving = lax.dynamic_index_in_dim(parts, core ^ bits, 0, keepdims=False)
        arrived = swap(after(leaving, facing, beyond), "sect", bits)
        other = arrived if other is None else other + arrived
    other = jnp.zeros_like(mine) if other is None else other
    weight = call(
        functools.partial(weight_kernel, plan),
        shape((plan.planes, plan.extent, ny), f32),
        [HBM] * 2 + [VMEM] * 2,
        [
            pltpu.SMEM(brightness.shape, f32),
            pltpu.VMEM(labels.shape, labels.dtype),
            pltpu.SemaphoreType.DMA((2,)),
        ],
    )(brightness, labels, facing, beyond)
    return call(
        functools.partial(blur_kernel, plan),
        shape((plan.planes, ny, plan.cz), f32),
        [VMEM] * 5,
    )(mine, other, weight, by, bz)


def solution(mesh):
    spread = P(("groups", "sect"), None, "tile")
    in_specs = (spread, spread, P("groups"), P(), P(), P(), P())
    return jax.shard_map(
        on_device, mesh=mesh, in_specs=in_specs, out_specs=spread, check_vma=False
    )
```

```python
import functools
import operator

import jax
import jax.numpy as jnp
from jax import lax
from jax.experimental import pallas as pl
from jax.experimental.pallas import tpu as pltpu
from jax.sharding import PartitionSpec as P

SHEET_WIDTH = 6.0
AMPLITUDE = 2.0
ROOM = 10 * 1024 * 1024
PIN = 1 << 40
SMEM = pltpu.SMEM
VMEM = pltpu.VMEM
HBM = pltpu.HBM


class Plan:
    def __init__(self, labels, positions, taps):
        self.planes, self.ny, self.cz = labels.shape
        self.half = taps // 2
        self.tiles = lax.axis_size("tile")
        self.cores = lax.axis_size("sect") // 2
        self.own = self.cores * self.planes
        self.all_x = 2 * self.own
        self.sheets = -(-positions // self.cores)
        self.block = 2 * self.half
        self.units = self.cz // self.half
        self.reach = -(-(self.all_x + 1) * self.half // self.cz)
        self.whole = self.tiles <= 2 * self.reach + 1
        self.window = self.tiles if self.whole else 2 * self.reach + 1
        self.rows = self.window * self.cz
        self.extent = self.cz + 2 * self.half
        self.width = self.sheets * self.ny

    def here(self):
        sect = lax.axis_index("sect")
        return lax.axis_index("tile"), sect // self.cores, lax.rem(sect, self.cores)

    def blocks(self, left):
        need = self.units + 2 + 2 * left
        return (min(need, self.window * self.units) if self.whole else need) // 2

    def start(self, left):
        left = operator.index(left)
        if self.whole:
            last = max(self.window * self.units - (self.units + 2 + 2 * left), 0)
            unit = 0 if last == 0 else jnp.clip(lax.axis_index("tile") * self.units - 1 - left, 0, last)
        else:
            unit = self.reach * self.units - 1 - left
        return unit * self.half

    def home(self):
        return lax.axis_index("tile") * self.cz if self.whole else self.reach * self.cz


def swap(x, axis, bits):
    count = lax.axis_size(axis)
    return lax.ppermute(x, axis, [(i, i ^ bits) for i in range(count)])


def shift(x, axis, step):
    count = lax.axis_size(axis)
    return lax.ppermute(x, axis, [(i, i + step) for i in range(count) if 0 <= i + step < count])


def after(x, *done):
    return lax.optimization_barrier((x, *done))[0]


def tile_pieces(plan, mine, crossed):
    if plan.whole and plan.tiles & (plan.tiles - 1) == 0:
        got = {0: mine}
        if plan.tiles == 4:
            got[3] = swap(mine, "tile", 3)
            got[1] = swap(mine, "tile", 1)
            got[2] = swap(after(got[3], got[1], *crossed), "tile", 1)
        else:
            for bits in range(1, plan.tiles):
                got[bits] = swap(mine, "tile", bits)
        return list(got.values()), [("xor", bits) for bits in got]
    if plan.whole:
        turns = range(plan.tiles)
        count = plan.tiles
        pieces = [
            lax.ppermute(mine, "tile", [(i, (i + k) % count) for i in range(count)]) if k else mine
            for k in turns
        ]
        return pieces, [("turn", k) for k in turns]
    steps = sorted(range(-plan.reach, plan.reach + 1), key=abs)
    return [shift(mine, "tile", -k) if k else mine for k in steps], [("step", k) for k in steps]


def block_of(plan, source):
    kind, k = source
    tile = lax.axis_index("tile")
    if kind == "xor":
        return tile ^ k, None
    if kind == "turn":
        return lax.rem(tile - k + plan.tiles, plan.tiles), None
    return k + plan.reach, (tile + k >= 0) & (tile + k < plan.tiles)


def aligned(row, size):
    return row if isinstance(row, int) else pl.multiple_of(row, size)


def halves(x):
    high = x.astype(jnp.bfloat16)
    return high, (x - high.astype(jnp.float32)).astype(jnp.bfloat16)


def dot(a, b):
    return jnp.dot(a, b, preferred_element_type=jnp.float32)


def three(high, low, matrix_high, matrix_low):
    return dot(high, matrix_high) + dot(low, matrix_high) + dot(high, matrix_low)


def circulant(row, size, half):
    wide = jnp.broadcast_to(row, (size, size))
    return pltpu.roll(wide, (size - half) % size, 1, stride=1, stride_axis=0).T


def band(row, size, wide):
    return pltpu.roll(jnp.broadcast_to(row, (size, wide)), 0, 1, stride=1, stride_axis=0)


def complex_matrix(diagonal, upper, lower):
    top = jnp.concatenate([diagonal, upper], axis=1)
    return jnp.concatenate([top, jnp.concatenate([lower, diagonal], axis=1)], axis=0)


def fetch(pairs, sems):
    copies = [pltpu.make_async_copy(src, dst, sems.at[i]) for i, (src, dst) in enumerate(pairs)]
    for copy in copies:
        copy.start()
    return copies


def prepare_kernel(plan, count, hbm_taps, hbm_dtaps, hbm_phases, hbm_positions, *refs):
    joined, refs = refs[:count], refs[count:]
    ky, kz, km, by, bz, table, sheet, together, taps, dtaps, phases, positions, line, sems = refs
    ny, half, block = plan.ny, plan.half, plan.block
    wide = 2 * block
    count = taps.shape[2]
    pairs = [(hbm_taps, taps), (hbm_dtaps, dtaps), (hbm_phases, phases), (hbm_positions, positions)]
    copies = fetch(pairs, sems)
    for number, piece in enumerate(joined):
        together[number * plan.planes:(number + 1) * plan.planes] = piece[...]
    for copy in copies:
        copy.wait()

    def padded(row):
        line[...] = jnp.zeros(line.shape, jnp.float32)
        line[0:1, :count] = row
        return line[0:1, :]

    def folded(row):
        spread = padded(row)
        return sum(spread[:, i:i + ny] for i in range(0, spread.shape[1], ny))

    def keep(ref, matrix, place=()):
        ref[(0, *place)], ref[(1, *place)] = halves(matrix)

    cyr = circulant(folded(taps[0, 0:1, :]), ny, half)
    cyi = circulant(folded(taps[0, 1:2, :]), ny, half)
    keep(ky, complex_matrix(cyr, cyi, -cyi))
    czr = band(padded(taps[1, 0:1, :])[:, :wide], block, wide)
    czi = band(padded(taps[1, 1:2, :])[:, :wide], block, wide)
    early = complex_matrix(czr[:, :block], -czi[:, :block], czi[:, :block])
    late = complex_matrix(czr[:, block:], -czi[:, block:], czi[:, block:])
    keep(kz, early, (0,))
    keep(kz, late, (1,))
    middle = early + late
    quarter = [
        [[middle[d:d + half, c + e:c + e + half] for c in (0, block)] for d in (0, block)] for e in (0, half)
    ]
    for number, sign in enumerate((1.0, -1.0)):
        part = jnp.concatenate(
            [jnp.concatenate([quarter[0][d][c] + sign * quarter[1][d][c] for c in range(2)], axis=1) for d in range(2)],
            axis=0,
        )
        high, low = halves(0.5 * part)
        km[number] = jnp.concatenate(
            [jnp.concatenate([high, high], axis=1), jnp.concatenate([low, low], axis=1)], axis=0
        )
    keep(by, circulant(folded(dtaps[0:1, :]), ny, half))
    keep(bz, band(padded(dtaps[1:2, :])[:, :wide], block, wide))

    table[0:1, :] = jnp.cos(phases[...])
    table[1:2, :] = jnp.sin(phases[...])
    core = plan.here()[2]
    lane = lax.broadcasted_iota(jnp.int32, (1, ny), 1).astype(jnp.float32)
    for p in range(plan.sheets):
        number = core * plan.sheets + p
        live = number < positions.shape[0]
        centre = positions[jnp.where(live, number, 0)].astype(jnp.float32)
        offset = (lane - centre) / SHEET_WIDTH
        sheet[:, p * ny:(p + 1) * ny] = jnp.where(live, AMPLITUDE, 0.0) * jnp.exp(-offset * offset)


def choose(index, values):
    size = 1 << (len(values) - 1).bit_length()
    values = list(values) + [values[-1]] * (size - len(values))
    for b in range(size.bit_length() - 1):
        bit = (index & (1 << b)) != 0
        values = [jnp.where(bit, values[i + 1], values[i]) for i in range(0, len(values), 2)]
    return values[0]


def look_up(plan, groups, pieces, table, cosine, sine):
    cz = plan.cz
    core = plan.here()[2]
    entries = [[table[part:part + 1, e:e + 1] for e in range(table.shape[1])] for part in range(2)]
    for number, piece in pieces:
        first = (core ^ (number % plan.cores)) * plan.planes
        for place, source in enumerate(groups[number // plan.cores]):
            block, valid = block_of(plan, source)
            row = pl.multiple_of(block * cz, cz)
            for plane in range(plan.planes):
                kind = piece[place * plan.planes + plane].T
                for values, target in zip(entries, (cosine, sine)):
                    value = choose(kind, values)
                    value = value if valid is None else jnp.where(valid, value, 0.0)
                    target[first + plane, pl.ds(row, cz), :] = value


def clear(plan, field, spread):
    half, rows = plan.half, plan.rows
    for ref in (field, spread):
        for d in range(2):
            ref[d, :half, :] = jnp.zeros((half, plan.width), jnp.float32)
            ref[d, half + rows:, :] = jnp.zeros((half, plan.width), jnp.float32)


def propagate(plan, cos_at, sin_at, left, sheet, ky, kz, km, field, spread):
    ny, half, block, sheets = plan.ny, plan.half, plan.block, plan.sheets
    source, target = plan.start(left + 1), plan.start(left)
    sources, targets = plan.blocks(left + 1), plan.blocks(left)

    def each(number, body):
        if plan.whole:
            for b in range(number):
                body(b)
        else:
            lax.fori_loop(0, number, lambda b, _: body(b), None)

    def turn(b):
        row = aligned(source + b * block, half)
        cos, sin = cos_at(row, block), sin_at(row, block)
        parts = []
        for p in range(sheets):
            lanes = slice(p * ny, (p + 1) * ny)
            if sheet is not None:
                plane = sheet[:, lanes]
                parts.append(jnp.concatenate([plane * cos, plane * sin], axis=1))
                continue
            re = field[0, pl.ds(row + half, block), lanes]
            im = field[1, pl.ds(row + half, block), lanes]
            parts.append(jnp.concatenate([re * cos - im * sin, re * sin + im * cos], axis=1))
        high, low = halves(jnp.concatenate(parts, axis=0))
        v = three(high, low, ky[0], ky[1])
        for d in range(2):
            spread[d, pl.ds(row + half, block), :] = jnp.concatenate(
                [v[p * block:(p + 1) * block, d * ny:(d + 1) * ny] for p in range(sheets)], axis=1
            )

    def product(number, x):
        high, low = halves(x)
        return dot(kz[0, number], high) + dot(kz[1, number], high) + dot(kz[0, number], low)

    def circular(x):
        top = jnp.concatenate([x[:half], x[block:block + half]], axis=0)
        bottom = jnp.concatenate([x[half:block], x[block + half:]], axis=0)
        sides = []
        for number, part in enumerate((top + bottom, top - bottom)):
            w = dot(km[number], jnp.concatenate(halves(part), axis=0))
            sides.append(w[:block] + w[block:])
        top, bottom = sides[0] + sides[1], sides[0] - sides[1]
        return jnp.concatenate([top[:half], bottom[:half], top[half:], bottom[half:]], axis=0)

    def window(row):
        return jnp.concatenate([spread[d, pl.ds(row, block), :] for d in range(2)], axis=0)

    def store(row, w):
        field[0, pl.ds(row + half, block), :] = w[:block]
        field[1, pl.ds(row + half, block), :] = w[block:]

    def pair(b):
        row = aligned(target + 2 * b * block, half)
        x = [window(row + i * block) for i in range(3)]
        shared = circular(x[1])
        store(row, product(0, x[0] - x[1]) + shared)
        store(row + block, product(1, x[2] - x[1]) + shared)

    def single(b):
        row = aligned(target + b * block, half)
        store(row, product(0, window(row)) + product(1, window(row + block)))

    each(sources, turn)
    each(targets // 2, pair)
    if targets % 2:
        single(targets - 1)


def energy(plan, field):
    home = pl.multiple_of(plan.home(), plan.half)
    re = field[0, pl.ds(home, plan.extent), :]
    im = field[1, pl.ds(home, plan.extent), :]
    every = re * re + im * im
    total = every[:, :plan.ny]
    for p in range(1, plan.sheets):
        total = total + every[:, p * plan.ny:(p + 1) * plan.ny]
    return total


def short_kernel(plan, groups, hbm_mine, ky, kz, km, table, sheet, *refs):
    count = len(groups) * plan.cores - 1
    pieces = refs[:count]
    out, hbm_cosine, hbm_sine, mine, cosine, sine, field, spread, sems = refs[count:]
    own = plan.own
    (arriving,) = fetch([(hbm_mine, mine)], sems)
    clear(plan, field, spread)
    look_up(plan, groups, list(enumerate(pieces, 1)), table, cosine, sine)
    arriving.wait()
    look_up(plan, groups, [(0, mine)], table, cosine, sine)
    leaving = fetch([(cosine, hbm_cosine), (sine, hbm_sine)], sems)
    side = plan.here()[1]

    def step(k, left):
        entering = None if k else sheet
        slot = jnp.where(side == 0, k, own - 1 - k)
        maps = [lambda row, n, ref=ref: ref[slot, pl.ds(row, n), :] for ref in (cosine, sine)]
        propagate(plan, *maps, left, entering, ky, kz, km, field, spread)
        out[slot] = energy(plan, field)

    for k in range(own):
        step(k, own - 1 - k)
    for copy in leaving:
        copy.wait()


def long_kernel(plan, groups, ky, kz, km, table, sheet, hbm_cosine, hbm_sine, earlier, *refs):
    count = len(groups) * plan.cores
    pieces = refs[:count]
    out, far_cosine, far_sine, cosine, sine, field, spread, sems = refs[count:]
    own = plan.own
    arriving = fetch([(hbm_cosine, cosine), (hbm_sine, sine)], sems)
    clear(plan, field, spread)
    look_up(plan, groups, list(enumerate(pieces)), table, far_cosine, far_sine)
    side = plan.here()[1]

    def far_step(k, left):
        entering = None if k else sheet
        slot = jnp.where(side == 0, own - 1 - k, k)
        maps = [lambda row, n, ref=ref: ref[slot, pl.ds(row, n), :] for ref in (far_cosine, far_sine)]
        propagate(plan, *maps, left, entering, ky, kz, km, field, spread)

    def step(k, left):
        entering = None
        slot = jnp.where(side == 0, 2 * own - 1 - k, k - own)
        maps = [lambda row, n, ref=ref: ref[slot, pl.ds(row, n), :] for ref in (cosine, sine)]
        propagate(plan, *maps, left, entering, ky, kz, km, field, spread)
        out[slot] = earlier[slot] + energy(plan, field)

    for k in range(own):
        far_step(k, 2 * own - 1 - k)
    for copy in arriving:
        copy.wait()
    for k in range(own, 2 * own):
        step(k, 2 * own - 1 - k)


def weight_kernel(plan, hbm_bright, hbm_labels, facing, beyond, weight, bright, labels, sems):
    half, ny, cz = plan.half, plan.ny, plan.cz
    first, arriving = fetch([(hbm_bright, bright), (hbm_labels, labels)], sems)
    first.wait()
    tile = lax.axis_index("tile")
    even = lax.rem(tile, 2) == 0
    first_half = lax.broadcasted_iota(jnp.int32, (ny, 2 * half), 1) < half
    ends = [(tile < plan.tiles - 1).astype(jnp.float32), (tile > 0).astype(jnp.float32)]
    inside = jnp.where(first_half, ends[0], ends[1])
    values = [bright[e] for e in range(bright.shape[0])]
    for x in range(plan.planes):
        before = jnp.where(even, beyond[x], facing[x])[:, -2 * half:]
        behind = jnp.where(even, facing[x], beyond[x])[:, :2 * half]
        halo = (choose(jnp.where(first_half, behind, before), values) * inside).T
        weight[x, :half, :] = halo[half:]
        weight[x, half + cz:, :] = halo[:half]
    arriving.wait()
    for x in range(plan.planes):
        weight[x, half:half + cz, :] = choose(labels[x], values).T


def blur_kernel(plan, mine, other, weight, by, bz, out):
    ny, extent, block = plan.ny, plan.extent, plan.block
    parts = [(mine[x] + other[x]) * weight[x] for x in range(plan.planes)]
    high, low = halves(jnp.concatenate(parts, axis=0))
    v = three(high, low, by[0], by[1])
    v = jnp.concatenate([v[x * extent:(x + 1) * extent] for x in range(plan.planes)], axis=1)
    high, low = halves(v)
    for b in range(plan.cz // block):
        rows = slice(b * block, b * block + 2 * block)
        w = dot(bz[0], high[rows]) + dot(bz[1], high[rows]) + dot(bz[0], low[rows])
        for x in range(plan.planes):
            out[x, :, b * block:(b + 1) * block] = w[:, x * ny:(x + 1) * ny].T


def size_of(x):
    return x.size * x.dtype.itemsize


def call(kernel, outs, in_spaces, scratch=(), flops=0, out_spaces=None):
    return lambda *args: call_with(args, kernel, outs, in_spaces, scratch, flops, out_spaces)


def call_with(args, kernel, outs, in_spaces, scratch, flops, out_spaces):
    args = [
        pltpu.with_memory_space_constraint(x, space) if space is HBM or size_of(x) > PIN else x
        for x, space in zip(args, in_spaces)
    ]
    held = [x for x, space in zip(args, in_spaces) if space is VMEM]
    held += jax.tree.leaves(outs)
    held += [jax.ShapeDtypeStruct(x.shape, x.dtype) for x in scratch if x.memory_space == VMEM]
    if out_spaces is None:
        out_spaces = jax.tree.map(lambda _: VMEM, outs)
    limit = ROOM + sum(size_of(x) for x in held)
    flat, tree = jax.tree.flatten(outs)
    spaces = jax.tree.leaves(out_spaces)
    outs = tree.unflatten(
        [HBM(x.shape, x.dtype) if space is HBM else x for x, space in zip(flat, spaces)]
    )
    return pl.pallas_call(
        kernel,
        out_shape=outs,
        in_specs=[pl.BlockSpec(memory_space=space) for space in in_spaces],
        out_specs=jax.tree.map(lambda space: pl.BlockSpec(memory_space=space), out_spaces),
        scratch_shapes=list(scratch),
        compiler_params=pltpu.CompilerParams(vmem_limit_bytes=limit),
        cost_estimate=pl.CostEstimate(flops=flops, bytes_accessed=1 << 20, transcendentals=0),
    )(*args)


def on_device(labels, classes, positions, phase_table, brightness, prop_taps, detect_taps):
    taps = prop_taps.shape[-1]
    plan = Plan(labels, positions.shape[0], taps)
    ny, half, block, rows = plan.ny, plan.half, plan.block, plan.rows
    tiles, cores = plan.tiles, plan.cores
    core = plan.here()[2]
    f32, bf16 = jnp.float32, jnp.bfloat16
    shape = jax.ShapeDtypeStruct

    def over_cores(array):
        return [array] + [swap(array, "sect", bits) for bits in range(1, cores)]

    crossed = [swap(classes, "sect", cores)]
    pieces, sources = tile_pieces(plan, classes, crossed)
    near = [over_cores(piece) for piece in pieces]
    joined = [after(pieces[1], *near[1][1:]), *pieces[2:-1]]
    near_groups = tuple((source,) for source in sources)
    far_groups = (sources[:1], sources[1:-1], sources[-1:])
    line = -(-max(4 * half, taps) // ny) * ny
    phases = phase_table[None]
    ky, kz, km, by, bz, table, sheet, together = call(
        functools.partial(prepare_kernel, plan, len(joined)),
        (
            shape((2, 2 * ny, 2 * ny), bf16),
            shape((2, 2, 2 * block, 2 * block), bf16),
            shape((2, 2 * block, 2 * block), bf16),
            shape((2, ny, ny), bf16),
            shape((2, block, 2 * block), bf16),
            shape((2, phases.shape[1]), f32),
            shape((1, plan.width), f32),
            shape((len(joined) * plan.planes, ny, plan.cz), classes.dtype),
        ),
        [HBM] * 4 + [VMEM] * len(joined),
        [
            pltpu.VMEM(prop_taps.shape, f32),
            pltpu.VMEM(detect_taps.shape, f32),
            pltpu.VMEM(phases.shape, f32),
            pltpu.SMEM(positions.shape, positions.dtype),
            pltpu.VMEM((8, line), f32),
            pltpu.SemaphoreType.DMA((4,)),
        ],
    )(prop_taps, detect_taps, phases, positions, *joined)
    near = sum(near, [])
    crossed += [swap(together, "sect", cores), swap(pieces[-1], "sect", cores)]

    maps = shape((plan.own, rows, ny), f32)
    whole_maps = pltpu.VMEM((plan.own, rows, ny), f32)
    state = pltpu.VMEM((2, rows + 2 * half, plan.width), f32)
    sums = shape((plan.own, plan.extent, ny), f32)
    sums, cosine, sine = call(
        functools.partial(short_kernel, plan, near_groups),
        (sums, maps, maps),
        [HBM] + [VMEM] * (4 + len(near)),
        [
            pltpu.VMEM(classes.shape, classes.dtype),
            whole_maps,
            whole_maps,
            state,
            state,
            pltpu.SemaphoreType.DMA((2,)),
        ],
        flops=1,
        out_spaces=(VMEM, HBM, HBM),
    )(near[0], ky, kz, km, table, sheet, *near[1:])

    pairs = [(i, i ^ 1) for i in range(tiles) if i ^ 1 < tiles]
    gaps = [(i, ((i + 1) ^ 1) - 1) for i in range(1, tiles) if ((i + 1) ^ 1) - 1 < tiles]
    if tiles == 4:
        gaps = [(i, i ^ 3) for i in range(tiles)]
    late = after(labels, sums)
    facing = lax.ppermute(late, "tile", pairs)
    beyond = lax.ppermute(late, "tile", gaps)

    far = []
    for piece in crossed:
        far += [piece] + over_cores(after(piece, sums))[1:]
    sums = call(
        functools.partial(long_kernel, plan, far_groups),
        shape((plan.own, plan.extent, ny), f32),
        [VMEM] * 5 + [HBM] * 2 + [VMEM] * (1 + len(far)),
        [whole_maps] * 4 + [state, state, pltpu.SemaphoreType.DMA((2,))],
        flops=6 * 10**9,
    )(ky, kz, km, table, sheet, cosine, sine, sums, *far)

    parts = sums.reshape(cores, plan.planes, plan.extent, ny)
    mine = lax.dynamic_index_in_dim(parts, core, 0, keepdims=False)
    other = None
    for bits in range(1, cores):
        leaving = lax.dynamic_index_in_dim(parts, core ^ bits, 0, keepdims=False)
        arrived = swap(after(leaving, facing, beyond), "sect", bits)
        other = arrived if other is None else other + arrived
    other = jnp.zeros_like(mine) if other is None else other
    weight = call(
        functools.partial(weight_kernel, plan),
        shape((plan.planes, plan.extent, ny), f32),
        [HBM] * 2 + [VMEM] * 2,
        [
            pltpu.SMEM(brightness.shape, f32),
            pltpu.VMEM(labels.shape, labels.dtype),
            pltpu.SemaphoreType.DMA((2,)),
        ],
    )(brightness, labels, facing, beyond)
    return call(
        functools.partial(blur_kernel, plan),
        shape((plan.planes, ny, plan.cz), f32),
        [VMEM] * 5,
    )(mine, other, weight, by, bz)


def solution(mesh):
    spread = P(("groups", "sect"), None, "tile")
    in_specs = (spread, spread, P("groups"), P(), P(), P(), P())
    return jax.shard_map(
        on_device, mesh=mesh, in_specs=in_specs, out_specs=spread, check_vma=False
    )
```

```python
import functools
import operator

import jax
import jax.numpy as jnp
from jax import lax
from jax.experimental import pallas as pl
from jax.experimental.pallas import tpu as pltpu
from jax.sharding import PartitionSpec as P

SHEET_WIDTH = 6.0
AMPLITUDE = 2.0
ROOM = 10 * 1024 * 1024
PIN = 1 << 40
SMEM = pltpu.SMEM
VMEM = pltpu.VMEM
HBM = pltpu.HBM


class Plan:
    def __init__(self, labels, positions, taps):
        self.planes, self.ny, self.cz = labels.shape
        self.half = taps // 2
        self.tiles = lax.axis_size("tile")
        self.cores = lax.axis_size("sect") // 2
        self.own = self.cores * self.planes
        self.all_x = 2 * self.own
        self.sheets = -(-positions // self.cores)
        self.block = 2 * self.half
        self.units = self.cz // self.half
        self.reach = -(-(self.all_x + 1) * self.half // self.cz)
        self.whole = self.tiles <= 2 * self.reach + 1
        self.window = self.tiles if self.whole else 2 * self.reach + 1
        self.rows = self.window * self.cz
        self.extent = self.cz + 2 * self.half
        self.width = self.sheets * self.ny

    def here(self):
        sect = lax.axis_index("sect")
        return lax.axis_index("tile"), sect // self.cores, lax.rem(sect, self.cores)

    def blocks(self, left):
        need = self.units + 2 + 2 * left
        return (min(need, self.window * self.units) if self.whole else need) // 2

    def start(self, left):
        left = operator.index(left)
        if self.whole:
            last = max(self.window * self.units - (self.units + 2 + 2 * left), 0)
            unit = 0 if last == 0 else jnp.clip(lax.axis_index("tile") * self.units - 1 - left, 0, last)
        else:
            unit = self.reach * self.units - 1 - left
        return unit * self.half

    def home(self):
        return lax.axis_index("tile") * self.cz if self.whole else self.reach * self.cz


def swap(x, axis, bits):
    count = lax.axis_size(axis)
    return lax.ppermute(x, axis, [(i, i ^ bits) for i in range(count)])


def shift(x, axis, step):
    count = lax.axis_size(axis)
    return lax.ppermute(x, axis, [(i, i + step) for i in range(count) if 0 <= i + step < count])


def after(x, *done):
    return lax.optimization_barrier((x, *done))[0]


def tile_pieces(plan, mine, crossed):
    if plan.whole and plan.tiles & (plan.tiles - 1) == 0:
        got = {0: mine}
        if plan.tiles == 4:
            got[3] = swap(mine, "tile", 3)
            got[1] = swap(mine, "tile", 1)
            got[2] = swap(after(got[3], got[1], *crossed), "tile", 1)
        else:
            for bits in range(1, plan.tiles):
                got[bits] = swap(mine, "tile", bits)
        return list(got.values()), [("xor", bits) for bits in got]
    if plan.whole:
        turns = range(plan.tiles)
        count = plan.tiles
        pieces = [
            lax.ppermute(mine, "tile", [(i, (i + k) % count) for i in range(count)]) if k else mine
            for k in turns
        ]
        return pieces, [("turn", k) for k in turns]
    steps = sorted(range(-plan.reach, plan.reach + 1), key=abs)
    return [shift(mine, "tile", -k) if k else mine for k in steps], [("step", k) for k in steps]


def block_of(plan, source):
    kind, k = source
    tile = lax.axis_index("tile")
    if kind == "xor":
        return tile ^ k, None
    if kind == "turn":
        return lax.rem(tile - k + plan.tiles, plan.tiles), None
    return k + plan.reach, (tile + k >= 0) & (tile + k < plan.tiles)


def aligned(row, size):
    return row if isinstance(row, int) else pl.multiple_of(row, size)


def halves(x):
    high = x.astype(jnp.bfloat16)
    return high, (x - high.astype(jnp.float32)).astype(jnp.bfloat16)


def dot(a, b):
    return jnp.dot(a, b, preferred_element_type=jnp.float32)


def three(high, low, matrix_high, matrix_low):
    return dot(high, matrix_high) + dot(low, matrix_high) + dot(high, matrix_low)


def circulant(row, size, half):
    wide = jnp.broadcast_to(row, (size, size))
    return pltpu.roll(wide, (size - half) % size, 1, stride=1, stride_axis=0).T


def band(row, size, wide):
    return pltpu.roll(jnp.broadcast_to(row, (size, wide)), 0, 1, stride=1, stride_axis=0)


def complex_matrix(diagonal, upper, lower):
    top = jnp.concatenate([diagonal, upper], axis=1)
    return jnp.concatenate([top, jnp.concatenate([lower, diagonal], axis=1)], axis=0)


def fetch(pairs, sems):
    copies = [pltpu.make_async_copy(src, dst, sems.at[i]) for i, (src, dst) in enumerate(pairs)]
    for copy in copies:
        copy.start()
    return copies


def prepare_kernel(plan, count, hbm_taps, hbm_dtaps, hbm_phases, hbm_positions, *refs):
    joined, refs = refs[:count], refs[count:]
    ky, kz, km, by, bz, table, sheet, together, taps, dtaps, phases, positions, line, sems = refs
    ny, half, block = plan.ny, plan.half, plan.block
    wide = 2 * block
    count = taps.shape[2]
    pairs = [(hbm_taps, taps), (hbm_dtaps, dtaps), (hbm_phases, phases), (hbm_positions, positions)]
    copies = fetch(pairs, sems)
    for number, piece in enumerate(joined):
        together[number * plan.planes:(number + 1) * plan.planes] = piece[...]
    for copy in copies:
        copy.wait()

    def padded(row):
        line[...] = jnp.zeros(line.shape, jnp.float32)
        line[0:1, :count] = row
        return line[0:1, :]

    def folded(row):
        spread = padded(row)
        return sum(spread[:, i:i + ny] for i in range(0, spread.shape[1], ny))

    def keep(ref, matrix, place=()):
        ref[(0, *place)], ref[(1, *place)] = halves(matrix)

    cyr = circulant(folded(taps[0, 0:1, :]), ny, half)
    cyi = circulant(folded(taps[0, 1:2, :]), ny, half)
    keep(ky, complex_matrix(cyr, cyi, -cyi))
    czr = band(padded(taps[1, 0:1, :])[:, :wide], block, wide)
    czi = band(padded(taps[1, 1:2, :])[:, :wide], block, wide)
    early = complex_matrix(czr[:, :block], -czi[:, :block], czi[:, :block])
    late = complex_matrix(czr[:, block:], -czi[:, block:], czi[:, block:])
    keep(kz, early, (0,))
    keep(kz, late, (1,))
    middle = early + late
    quarter = [
        [[middle[d:d + half, c + e:c + e + half] for c in (0, block)] for d in (0, block)] for e in (0, half)
    ]
    for number, sign in enumerate((1.0, -1.0)):
        part = jnp.concatenate(
            [jnp.concatenate([quarter[0][d][c] + sign * quarter[1][d][c] for c in range(2)], axis=1) for d in range(2)],
            axis=0,
        )
        high, low = halves(0.5 * part)
        km[number] = jnp.concatenate(
            [jnp.concatenate([high, high], axis=1), jnp.concatenate([low, low], axis=1)], axis=0
        )
    keep(by, circulant(folded(dtaps[0:1, :]), ny, half))
    keep(bz, band(padded(dtaps[1:2, :])[:, :wide], block, wide))

    number = phases.shape[1]
    for part, row in enumerate((jnp.cos(phases[...]), jnp.sin(phases[...]))):
        for e in range(number):
            place = part * number + e
            table[place:place + 1, :] = jnp.broadcast_to(row[:, e:e + 1], (1, table.shape[1]))
    core = plan.here()[2]
    lane = lax.broadcasted_iota(jnp.int32, (1, ny), 1).astype(jnp.float32)
    for p in range(plan.sheets):
        number = core * plan.sheets + p
        live = number < positions.shape[0]
        centre = positions[jnp.where(live, number, 0)].astype(jnp.float32)
        offset = (lane - centre) / SHEET_WIDTH
        sheet[:, p * ny:(p + 1) * ny] = jnp.where(live, AMPLITUDE, 0.0) * jnp.exp(-offset * offset)


def choose(index, *tables):
    count = len(tables[0])
    size = 1 << (count - 1).bit_length()
    tables = [list(values) + [values[-1]] * (size - count) for values in tables]
    for b in range(size.bit_length() - 1):
        bit = (index & (1 << b)) != 0
        tables = [
            [jnp.where(bit, values[i + 1], values[i]) for i in range(0, len(values), 2)] for values in tables
        ]
    return [values[0] for values in tables]


def look_up(plan, groups, pieces, table, cosine, sine):
    cz = plan.cz
    core = plan.here()[2]
    count = table.shape[0] // 2
    entries = [[table[part * count + e:part * count + e + 1, :] for e in range(count)] for part in range(2)]
    for number, piece in pieces:
        first = (core ^ (number % plan.cores)) * plan.planes
        for place, source in enumerate(groups[number // plan.cores]):
            block, valid = block_of(plan, source)
            row = pl.multiple_of(block * cz, cz)
            for plane in range(plan.planes):
                kind = piece[place * plan.planes + plane].T
                for value, target in zip(choose(kind, *entries), (cosine, sine)):
                    value = value if valid is None else jnp.where(valid, value, 0.0)
                    target[first + plane, pl.ds(row, cz), :] = value


def clear(plan, field, spread):
    half, rows = plan.half, plan.rows
    for ref in (field, spread):
        for d in range(2):
            ref[d, :half, :] = jnp.zeros((half, plan.width), jnp.float32)
            ref[d, half + rows:, :] = jnp.zeros((half, plan.width), jnp.float32)


def propagate(plan, cos_at, sin_at, left, sheet, ky, kz, km, field, spread):
    ny, half, block, sheets = plan.ny, plan.half, plan.block, plan.sheets
    source, target = plan.start(left + 1), plan.start(left)
    sources, targets = plan.blocks(left + 1), plan.blocks(left)

    def each(number, body):
        if plan.whole:
            for b in range(number):
                body(b)
        else:
            lax.fori_loop(0, number, lambda b, _: body(b), None)

    def turn(b):
        row = aligned(source + b * block, half)
        cos, sin = cos_at(row, block), sin_at(row, block)
        parts = []
        for p in range(sheets):
            lanes = slice(p * ny, (p + 1) * ny)
            if sheet is not None:
                plane = sheet[:, lanes]
                parts.append(jnp.concatenate([plane * cos, plane * sin], axis=1))
                continue
            re = field[0, pl.ds(row + half, block), lanes]
            im = field[1, pl.ds(row + half, block), lanes]
            parts.append(jnp.concatenate([re * cos - im * sin, re * sin + im * cos], axis=1))
        high, low = halves(jnp.concatenate(parts, axis=0))
        v = three(high, low, ky[0], ky[1])
        for d in range(2):
            spread[d, pl.ds(row + half, block), :] = jnp.concatenate(
                [v[p * block:(p + 1) * block, d * ny:(d + 1) * ny] for p in range(sheets)], axis=1
            )

    def product(number, x):
        high, low = halves(x)
        return dot(kz[0, number], high) + dot(kz[1, number], high) + dot(kz[0, number], low)

    def circular(x):
        top = jnp.concatenate([x[:half], x[block:block + half]], axis=0)
        bottom = jnp.concatenate([x[half:block], x[block + half:]], axis=0)
        sides = []
        for number, part in enumerate((top + bottom, top - bottom)):
            w = dot(km[number], jnp.concatenate(halves(part), axis=0))
            sides.append(w[:block] + w[block:])
        top, bottom = sides[0] + sides[1], sides[0] - sides[1]
        return jnp.concatenate([top[:half], bottom[:half], top[half:], bottom[half:]], axis=0)

    def window(row):
        return jnp.concatenate([spread[d, pl.ds(row, block), :] for d in range(2)], axis=0)

    def store(row, w):
        field[0, pl.ds(row + half, block), :] = w[:block]
        field[1, pl.ds(row + half, block), :] = w[block:]

    def pair(b):
        row = aligned(target + 2 * b * block, half)
        x = [window(row + i * block) for i in range(3)]
        shared = circular(x[1])
        store(row, product(0, x[0] - x[1]) + shared)
        store(row + block, product(1, x[2] - x[1]) + shared)

    def single(b):
        row = aligned(target + b * block, half)
        store(row, product(0, window(row)) + product(1, window(row + block)))

    each(sources, turn)
    each(targets // 2, pair)
    if targets % 2:
        single(targets - 1)


def energy(plan, field):
    home = pl.multiple_of(plan.home(), plan.half)
    re = field[0, pl.ds(home, plan.extent), :]
    im = field[1, pl.ds(home, plan.extent), :]
    every = re * re + im * im
    total = every[:, :plan.ny]
    for p in range(1, plan.sheets):
        total = total + every[:, p * plan.ny:(p + 1) * plan.ny]
    return total


def short_kernel(plan, groups, mine, ky, kz, km, table, sheet, *refs):
    count = len(groups) * plan.cores - 1
    pieces = refs[:count]
    out, hbm_cosine, hbm_sine, cosine, sine, field, spread, sems = refs[count:]
    own = plan.own
    clear(plan, field, spread)
    look_up(plan, groups, list(enumerate(pieces, 1)), table, cosine, sine)
    look_up(plan, groups, [(0, mine)], table, cosine, sine)
    leaving = fetch([(cosine, hbm_cosine), (sine, hbm_sine)], sems)
    side = plan.here()[1]

    def step(k, left):
        entering = None if k else sheet
        slot = jnp.where(side == 0, k, own - 1 - k)
        maps = [lambda row, n, ref=ref: ref[slot, pl.ds(row, n), :] for ref in (cosine, sine)]
        propagate(plan, *maps, left, entering, ky, kz, km, field, spread)
        out[slot] = energy(plan, field)

    for k in range(own):
        step(k, own - 1 - k)
    for copy in leaving:
        copy.wait()


def long_kernel(plan, groups, ky, kz, km, table, sheet, hbm_cosine, hbm_sine, earlier, *refs):
    count = len(groups) * plan.cores
    pieces = refs[:count]
    out, far_cosine, far_sine, cosine, sine, field, spread, sems = refs[count:]
    own = plan.own
    arriving = fetch([(hbm_cosine, cosine), (hbm_sine, sine)], sems)
    clear(plan, field, spread)
    look_up(plan, groups, list(enumerate(pieces)), table, far_cosine, far_sine)
    side = plan.here()[1]

    def far_step(k, left):
        entering = None if k else sheet
        slot = jnp.where(side == 0, own - 1 - k, k)
        maps = [lambda row, n, ref=ref: ref[slot, pl.ds(row, n), :] for ref in (far_cosine, far_sine)]
        propagate(plan, *maps, left, entering, ky, kz, km, field, spread)

    def step(k, left):
        entering = None
        slot = jnp.where(side == 0, 2 * own - 1 - k, k - own)
        maps = [lambda row, n, ref=ref: ref[slot, pl.ds(row, n), :] for ref in (cosine, sine)]
        propagate(plan, *maps, left, entering, ky, kz, km, field, spread)
        out[slot] = earlier[slot] + energy(plan, field)

    for k in range(own):
        far_step(k, 2 * own - 1 - k)
    for copy in arriving:
        copy.wait()
    for k in range(own, 2 * own):
        step(k, 2 * own - 1 - k)


def weight_kernel(plan, hbm_bright, hbm_labels, facing, beyond, weight, bright, labels, sems):
    half, ny, cz = plan.half, plan.ny, plan.cz
    first, arriving = fetch([(hbm_bright, bright), (hbm_labels, labels)], sems)
    first.wait()
    tile = lax.axis_index("tile")
    even = lax.rem(tile, 2) == 0
    first_half = lax.broadcasted_iota(jnp.int32, (ny, 2 * half), 1) < half
    ends = [(tile < plan.tiles - 1).astype(jnp.float32), (tile > 0).astype(jnp.float32)]
    inside = jnp.where(first_half, ends[0], ends[1])
    values = [bright[e] for e in range(bright.shape[0])]
    for x in range(plan.planes):
        before = jnp.where(even, beyond[x], facing[x])[:, -2 * half:]
        behind = jnp.where(even, facing[x], beyond[x])[:, :2 * half]
        halo = (choose(jnp.where(first_half, behind, before), values)[0] * inside).T
        weight[x, :half, :] = halo[half:]
        weight[x, half + cz:, :] = halo[:half]
    arriving.wait()
    for x in range(plan.planes):
        weight[x, half:half + cz, :] = choose(labels[x], values)[0].T


def blur_kernel(plan, mine, other, weight, by, bz, out):
    ny, extent, block = plan.ny, plan.extent, plan.block
    parts = [(mine[x] + other[x]) * weight[x] for x in range(plan.planes)]
    high, low = halves(jnp.concatenate(parts, axis=0))
    v = three(high, low, by[0], by[1])
    v = jnp.concatenate([v[x * extent:(x + 1) * extent] for x in range(plan.planes)], axis=1)
    high, low = halves(v)
    for b in range(plan.cz // block):
        rows = slice(b * block, b * block + 2 * block)
        w = dot(bz[0], high[rows]) + dot(bz[1], high[rows]) + dot(bz[0], low[rows])
        for x in range(plan.planes):
            out[x, :, b * block:(b + 1) * block] = w[:, x * ny:(x + 1) * ny].T


def size_of(x):
    return x.size * x.dtype.itemsize


def call(kernel, outs, in_spaces, scratch=(), flops=0, out_spaces=None):
    return lambda *args: call_with(args, kernel, outs, in_spaces, scratch, flops, out_spaces)


def call_with(args, kernel, outs, in_spaces, scratch, flops, out_spaces):
    args = [
        pltpu.with_memory_space_constraint(x, space) if space is HBM or size_of(x) > PIN else x
        for x, space in zip(args, in_spaces)
    ]
    held = [x for x, space in zip(args, in_spaces) if space is VMEM]
    held += jax.tree.leaves(outs)
    held += [jax.ShapeDtypeStruct(x.shape, x.dtype) for x in scratch if x.memory_space == VMEM]
    if out_spaces is None:
        out_spaces = jax.tree.map(lambda _: VMEM, outs)
    limit = ROOM + sum(size_of(x) for x in held)
    flat, tree = jax.tree.flatten(outs)
    spaces = jax.tree.leaves(out_spaces)
    outs = tree.unflatten(
        [HBM(x.shape, x.dtype) if space is HBM else x for x, space in zip(flat, spaces)]
    )
    return pl.pallas_call(
        kernel,
        out_shape=outs,
        in_specs=[pl.BlockSpec(memory_space=space) for space in in_spaces],
        out_specs=jax.tree.map(lambda space: pl.BlockSpec(memory_space=space), out_spaces),
        scratch_shapes=list(scratch),
        compiler_params=pltpu.CompilerParams(vmem_limit_bytes=limit),
        cost_estimate=pl.CostEstimate(flops=flops, bytes_accessed=1 << 20, transcendentals=0),
    )(*args)


def on_device(labels, classes, positions, phase_table, brightness, prop_taps, detect_taps):
    taps = prop_taps.shape[-1]
    plan = Plan(labels, positions.shape[0], taps)
    ny, half, block, rows = plan.ny, plan.half, plan.block, plan.rows
    tiles, cores = plan.tiles, plan.cores
    core = plan.here()[2]
    f32, bf16 = jnp.float32, jnp.bfloat16
    shape = jax.ShapeDtypeStruct

    def over_cores(array):
        return [array] + [swap(array, "sect", bits) for bits in range(1, cores)]

    crossed = [swap(classes, "sect", cores)]
    pieces, sources = tile_pieces(plan, classes, crossed)
    near = [over_cores(piece) for piece in pieces]
    joined = [after(pieces[1], *near[1][1:]), *pieces[2:-1]]
    near_groups = tuple((source,) for source in sources)
    far_groups = (sources[:1], sources[1:-1], sources[-1:])
    line = -(-max(4 * half, taps) // ny) * ny
    phases = phase_table[None]
    ky, kz, km, by, bz, table, sheet, together = call(
        functools.partial(prepare_kernel, plan, len(joined)),
        (
            shape((2, 2 * ny, 2 * ny), bf16),
            shape((2, 2, 2 * block, 2 * block), bf16),
            shape((2, 2 * block, 2 * block), bf16),
            shape((2, ny, ny), bf16),
            shape((2, block, 2 * block), bf16),
            shape((2 * phases.shape[1], ny), f32),
            shape((1, plan.width), f32),
            shape((len(joined) * plan.planes, ny, plan.cz), classes.dtype),
        ),
        [HBM] * 4 + [VMEM] * len(joined),
        [
            pltpu.VMEM(prop_taps.shape, f32),
            pltpu.VMEM(detect_taps.shape, f32),
            pltpu.VMEM(phases.shape, f32),
            pltpu.SMEM(positions.shape, positions.dtype),
            pltpu.VMEM((8, line), f32),
            pltpu.SemaphoreType.DMA((4,)),
        ],
    )(prop_taps, detect_taps, phases, positions, *joined)
    near = sum(near, [])
    crossed += [swap(together, "sect", cores), swap(pieces[-1], "sect", cores)]

    maps = shape((plan.own, rows, ny), f32)
    whole_maps = pltpu.VMEM((plan.own, rows, ny), f32)
    state = pltpu.VMEM((2, rows + 2 * half, plan.width), f32)
    sums = shape((plan.own, plan.extent, ny), f32)
    sums, cosine, sine = call(
        functools.partial(short_kernel, plan, near_groups),
        (sums, maps, maps),
        [VMEM] * (5 + len(near)),
        [
            whole_maps,
            whole_maps,
            state,
            state,
            pltpu.SemaphoreType.DMA((2,)),
        ],
        flops=1,
        out_spaces=(VMEM, HBM, HBM),
    )(near[0], ky, kz, km, table, sheet, *near[1:])

    pairs = [(i, i ^ 1) for i in range(tiles) if i ^ 1 < tiles]
    gaps = [(i, ((i + 1) ^ 1) - 1) for i in range(1, tiles) if ((i + 1) ^ 1) - 1 < tiles]
    if tiles == 4:
        gaps = [(i, i ^ 3) for i in range(tiles)]
    late = after(labels, sums)
    facing = lax.ppermute(late, "tile", pairs)
    beyond = lax.ppermute(late, "tile", gaps)

    far = []
    for piece in crossed:
        far += [piece] + over_cores(after(piece, sums))[1:]
    sums = call(
        functools.partial(long_kernel, plan, far_groups),
        shape((plan.own, plan.extent, ny), f32),
        [VMEM] * 5 + [HBM] * 2 + [VMEM] * (1 + len(far)),
        [whole_maps] * 4 + [state, state, pltpu.SemaphoreType.DMA((2,))],
        flops=6 * 10**9,
    )(ky, kz, km, table, sheet, cosine, sine, sums, *far)

    parts = sums.reshape(cores, plan.planes, plan.extent, ny)
    mine = lax.dynamic_index_in_dim(parts, core, 0, keepdims=False)
    other = None
    for bits in range(1, cores):
        leaving = lax.dynamic_index_in_dim(parts, core ^ bits, 0, keepdims=False)
        arrived = swap(after(leaving, facing, beyond), "sect", bits)
        other = arrived if other is None else other + arrived
    other = jnp.zeros_like(mine) if other is None else other
    weight = call(
        functools.partial(weight_kernel, plan),
        shape((plan.planes, plan.extent, ny), f32),
        [HBM] * 2 + [VMEM] * 2,
        [
            pltpu.SMEM(brightness.shape, f32),
            pltpu.VMEM(labels.shape, labels.dtype),
            pltpu.SemaphoreType.DMA((2,)),
        ],
    )(brightness, labels, facing, beyond)
    return call(
        functools.partial(blur_kernel, plan),
        shape((plan.planes, ny, plan.cz), f32),
        [VMEM] * 5,
    )(mine, other, weight, by, bz)


def solution(mesh):
    spread = P(("groups", "sect"), None, "tile")
    in_specs = (spread, spread, P("groups"), P(), P(), P(), P())
    return jax.shard_map(
        on_device, mesh=mesh, in_specs=in_specs, out_specs=spread, check_vma=False
    )
```

```python
import functools
import operator

import jax
import jax.numpy as jnp
from jax import lax
from jax.experimental import pallas as pl
from jax.experimental.pallas import tpu as pltpu
from jax.sharding import PartitionSpec as P

SHEET_WIDTH = 6.0
AMPLITUDE = 2.0
ROOM = 10 * 1024 * 1024
PIN = 1 << 40
SMEM = pltpu.SMEM
VMEM = pltpu.VMEM
HBM = pltpu.HBM


class Plan:
    def __init__(self, labels, positions, taps):
        self.planes, self.ny, self.cz = labels.shape
        self.half = taps // 2
        self.tiles = lax.axis_size("tile")
        self.cores = lax.axis_size("sect") // 2
        self.own = self.cores * self.planes
        self.all_x = 2 * self.own
        self.sheets = -(-positions // self.cores)
        self.block = 2 * self.half
        self.units = self.cz // self.half
        self.reach = -(-(self.all_x + 1) * self.half // self.cz)
        self.whole = self.tiles <= 2 * self.reach + 1
        self.window = self.tiles if self.whole else 2 * self.reach + 1
        self.rows = self.window * self.cz
        self.extent = self.cz + 2 * self.half
        self.width = self.sheets * self.ny

    def here(self):
        sect = lax.axis_index("sect")
        return lax.axis_index("tile"), sect // self.cores, lax.rem(sect, self.cores)

    def blocks(self, left):
        need = self.units + 2 + 2 * left
        return (min(need, self.window * self.units) if self.whole else need) // 2

    def start(self, left):
        left = operator.index(left)
        if self.whole:
            last = max(self.window * self.units - (self.units + 2 + 2 * left), 0)
            unit = 0 if last == 0 else jnp.clip(lax.axis_index("tile") * self.units - 1 - left, 0, last)
        else:
            unit = self.reach * self.units - 1 - left
        return unit * self.half

    def home(self):
        return lax.axis_index("tile") * self.cz if self.whole else self.reach * self.cz


def swap(x, axis, bits):
    count = lax.axis_size(axis)
    return lax.ppermute(x, axis, [(i, i ^ bits) for i in range(count)])


def shift(x, axis, step):
    count = lax.axis_size(axis)
    return lax.ppermute(x, axis, [(i, i + step) for i in range(count) if 0 <= i + step < count])


def after(x, *done):
    return lax.optimization_barrier((x, *done))[0]


def tile_pieces(plan, mine, crossed):
    if plan.whole and plan.tiles & (plan.tiles - 1) == 0:
        got = {0: mine}
        if plan.tiles == 4:
            got[3] = swap(mine, "tile", 3)
            got[1] = swap(mine, "tile", 1)
            got[2] = swap(after(got[3], got[1], *crossed), "tile", 1)
        else:
            for bits in range(1, plan.tiles):
                got[bits] = swap(mine, "tile", bits)
        return list(got.values()), [("xor", bits) for bits in got]
    if plan.whole:
        turns = range(plan.tiles)
        count = plan.tiles
        pieces = [
            lax.ppermute(mine, "tile", [(i, (i + k) % count) for i in range(count)]) if k else mine
            for k in turns
        ]
        return pieces, [("turn", k) for k in turns]
    steps = sorted(range(-plan.reach, plan.reach + 1), key=abs)
    return [shift(mine, "tile", -k) if k else mine for k in steps], [("step", k) for k in steps]


def block_of(plan, source):
    kind, k = source
    tile = lax.axis_index("tile")
    if kind == "xor":
        return tile ^ k, None
    if kind == "turn":
        return lax.rem(tile - k + plan.tiles, plan.tiles), None
    return k + plan.reach, (tile + k >= 0) & (tile + k < plan.tiles)


def aligned(row, size):
    return row if isinstance(row, int) else pl.multiple_of(row, size)


def halves(x):
    high = x.astype(jnp.bfloat16)
    return high, (x - high.astype(jnp.float32)).astype(jnp.bfloat16)


def dot(a, b):
    return jnp.dot(a, b, preferred_element_type=jnp.float32)


def three(high, low, matrix_high, matrix_low):
    return dot(high, matrix_high) + dot(low, matrix_high) + dot(high, matrix_low)


def circulant(row, size, half):
    wide = jnp.broadcast_to(row, (size, size))
    return pltpu.roll(wide, (size - half) % size, 1, stride=1, stride_axis=0).T


def band(row, size, wide):
    return pltpu.roll(jnp.broadcast_to(row, (size, wide)), 0, 1, stride=1, stride_axis=0)


def complex_matrix(diagonal, upper, lower):
    top = jnp.concatenate([diagonal, upper], axis=1)
    return jnp.concatenate([top, jnp.concatenate([lower, diagonal], axis=1)], axis=0)


def fetch(pairs, sems):
    copies = [pltpu.make_async_copy(src, dst, sems.at[i]) for i, (src, dst) in enumerate(pairs)]
    for copy in copies:
        copy.start()
    return copies


def tap_rows(ny, line):
    def padded(row):
        line[...] = jnp.zeros(line.shape, jnp.float32)
        line[0:1, :row.shape[1]] = row
        return line[0:1, :]

    def folded(row):
        spread = padded(row)
        return sum(spread[:, i:i + ny] for i in range(0, spread.shape[1], ny))

    return padded, folded


def keep(ref, matrix, place=()):
    ref[(0, *place)], ref[(1, *place)] = halves(matrix)


def prepare_kernel(plan, count, hbm_taps, hbm_phases, hbm_positions, *refs):
    joined, refs = refs[:count], refs[count:]
    ky, kz, km, table, sheet, together, taps, phases, positions, line, sems = refs
    ny, half, block = plan.ny, plan.half, plan.block
    wide = 2 * block
    pairs = [(hbm_taps, taps), (hbm_phases, phases), (hbm_positions, positions)]
    copies = fetch(pairs, sems)
    for number, piece in enumerate(joined):
        together[number * plan.planes:(number + 1) * plan.planes] = piece[...]
    for copy in copies:
        copy.wait()

    padded, folded = tap_rows(ny, line)

    cyr = circulant(folded(taps[0, 0:1, :]), ny, half)
    cyi = circulant(folded(taps[0, 1:2, :]), ny, half)
    keep(ky, complex_matrix(cyr, cyi, -cyi))
    czr = band(padded(taps[1, 0:1, :])[:, :wide], block, wide)
    czi = band(padded(taps[1, 1:2, :])[:, :wide], block, wide)
    early = complex_matrix(czr[:, :block], -czi[:, :block], czi[:, :block])
    late = complex_matrix(czr[:, block:], -czi[:, block:], czi[:, block:])
    keep(kz, early, (0,))
    keep(kz, late, (1,))
    middle = early + late
    quarter = [
        [[middle[d:d + half, c + e:c + e + half] for c in (0, block)] for d in (0, block)] for e in (0, half)
    ]
    for number, sign in enumerate((1.0, -1.0)):
        part = jnp.concatenate(
            [jnp.concatenate([quarter[0][d][c] + sign * quarter[1][d][c] for c in range(2)], axis=1) for d in range(2)],
            axis=0,
        )
        high, low = halves(0.5 * part)
        km[number] = jnp.concatenate(
            [jnp.concatenate([high, high], axis=1), jnp.concatenate([low, low], axis=1)], axis=0
        )

    number = phases.shape[1]
    for part, row in enumerate((jnp.cos(phases[...]), jnp.sin(phases[...]))):
        for e in range(number):
            place = part * number + e
            table[place:place + 1, :] = jnp.broadcast_to(row[:, e:e + 1], (1, table.shape[1]))
    core = plan.here()[2]
    lane = lax.broadcasted_iota(jnp.int32, (1, ny), 1).astype(jnp.float32)
    for p in range(plan.sheets):
        number = core * plan.sheets + p
        live = number < positions.shape[0]
        centre = positions[jnp.where(live, number, 0)].astype(jnp.float32)
        offset = (lane - centre) / SHEET_WIDTH
        sheet[:, p * ny:(p + 1) * ny] = jnp.where(live, AMPLITUDE, 0.0) * jnp.exp(-offset * offset)


def choose(index, *tables):
    count = len(tables[0])
    size = 1 << (count - 1).bit_length()
    tables = [list(values) + [values[-1]] * (size - count) for values in tables]
    for b in range(size.bit_length() - 1):
        bit = (index & (1 << b)) != 0
        tables = [
            [jnp.where(bit, values[i + 1], values[i]) for i in range(0, len(values), 2)] for values in tables
        ]
    return [values[0] for values in tables]


def look_up(plan, groups, pieces, table, cosine, sine):
    cz = plan.cz
    core = plan.here()[2]
    count = table.shape[0] // 2
    entries = [[table[part * count + e:part * count + e + 1, :] for e in range(count)] for part in range(2)]
    for number, piece in pieces:
        first = (core ^ (number % plan.cores)) * plan.planes
        for place, source in enumerate(groups[number // plan.cores]):
            block, valid = block_of(plan, source)
            row = pl.multiple_of(block * cz, cz)
            for plane in range(plan.planes):
                kind = piece[place * plan.planes + plane].T
                for value, target in zip(choose(kind, *entries), (cosine, sine)):
                    value = value if valid is None else jnp.where(valid, value, 0.0)
                    target[first + plane, pl.ds(row, cz), :] = value


def clear(plan, field, spread):
    half, rows = plan.half, plan.rows
    for ref in (field, spread):
        for d in range(2):
            ref[d, :half, :] = jnp.zeros((half, plan.width), jnp.float32)
            ref[d, half + rows:, :] = jnp.zeros((half, plan.width), jnp.float32)


def propagate(plan, cos_at, sin_at, left, sheet, ky, kz, km, field, spread):
    ny, half, block, sheets = plan.ny, plan.half, plan.block, plan.sheets
    source, target = plan.start(left + 1), plan.start(left)
    sources, targets = plan.blocks(left + 1), plan.blocks(left)

    def each(number, body):
        if plan.whole:
            for b in range(number):
                body(b)
        else:
            lax.fori_loop(0, number, lambda b, _: body(b), None)

    def turn(b):
        row = aligned(source + b * block, half)
        cos, sin = cos_at(row, block), sin_at(row, block)
        parts = []
        for p in range(sheets):
            lanes = slice(p * ny, (p + 1) * ny)
            if sheet is not None:
                plane = sheet[:, lanes]
                parts.append(jnp.concatenate([plane * cos, plane * sin], axis=1))
                continue
            re = field[0, pl.ds(row + half, block), lanes]
            im = field[1, pl.ds(row + half, block), lanes]
            parts.append(jnp.concatenate([re * cos - im * sin, re * sin + im * cos], axis=1))
        high, low = halves(jnp.concatenate(parts, axis=0))
        v = three(high, low, ky[0], ky[1])
        for d in range(2):
            spread[d, pl.ds(row + half, block), :] = jnp.concatenate(
                [v[p * block:(p + 1) * block, d * ny:(d + 1) * ny] for p in range(sheets)], axis=1
            )

    def product(number, x):
        high, low = halves(x)
        return dot(kz[0, number], high) + dot(kz[1, number], high) + dot(kz[0, number], low)

    def circular(x):
        top = jnp.concatenate([x[:half], x[block:block + half]], axis=0)
        bottom = jnp.concatenate([x[half:block], x[block + half:]], axis=0)
        sides = []
        for number, part in enumerate((top + bottom, top - bottom)):
            w = dot(km[number], jnp.concatenate(halves(part), axis=0))
            sides.append(w[:block] + w[block:])
        top, bottom = sides[0] + sides[1], sides[0] - sides[1]
        return jnp.concatenate([top[:half], bottom[:half], top[half:], bottom[half:]], axis=0)

    def window(row):
        return jnp.concatenate([spread[d, pl.ds(row, block), :] for d in range(2)], axis=0)

    def store(row, w):
        field[0, pl.ds(row + half, block), :] = w[:block]
        field[1, pl.ds(row + half, block), :] = w[block:]

    def pair(b):
        row = aligned(target + 2 * b * block, half)
        x = [window(row + i * block) for i in range(3)]
        shared = circular(x[1])
        store(row, product(0, x[0] - x[1]) + shared)
        store(row + block, product(1, x[2] - x[1]) + shared)

    def single(b):
        row = aligned(target + b * block, half)
        store(row, product(0, window(row)) + product(1, window(row + block)))

    each(sources, turn)
    each(targets // 2, pair)
    if targets % 2:
        single(targets - 1)


def energy(plan, field):
    home = pl.multiple_of(plan.home(), plan.half)
    re = field[0, pl.ds(home, plan.extent), :]
    im = field[1, pl.ds(home, plan.extent), :]
    every = re * re + im * im
    total = every[:, :plan.ny]
    for p in range(1, plan.sheets):
        total = total + every[:, p * plan.ny:(p + 1) * plan.ny]
    return total


def short_kernel(plan, groups, mine, ky, kz, km, table, sheet, *refs):
    count = len(groups) * plan.cores - 1
    pieces = refs[:count]
    out, hbm_cosine, hbm_sine, cosine, sine, field, spread, sems = refs[count:]
    own = plan.own
    clear(plan, field, spread)
    look_up(plan, groups, list(enumerate(pieces, 1)), table, cosine, sine)
    look_up(plan, groups, [(0, mine)], table, cosine, sine)
    leaving = fetch([(cosine, hbm_cosine), (sine, hbm_sine)], sems)
    side = plan.here()[1]

    def step(k, left):
        entering = None if k else sheet
        slot = jnp.where(side == 0, k, own - 1 - k)
        maps = [lambda row, n, ref=ref: ref[slot, pl.ds(row, n), :] for ref in (cosine, sine)]
        propagate(plan, *maps, left, entering, ky, kz, km, field, spread)
        out[slot] = energy(plan, field)

    for k in range(own):
        step(k, own - 1 - k)
    for copy in leaving:
        copy.wait()


def long_kernel(plan, groups, ky, kz, km, table, sheet, hbm_cosine, hbm_sine, earlier, *refs):
    count = len(groups) * plan.cores
    pieces = refs[:count]
    out, far_cosine, far_sine, cosine, sine, field, spread, sems = refs[count:]
    own = plan.own
    arriving = fetch([(hbm_cosine, cosine), (hbm_sine, sine)], sems)
    clear(plan, field, spread)
    look_up(plan, groups, list(enumerate(pieces)), table, far_cosine, far_sine)
    side = plan.here()[1]

    def far_step(k, left):
        entering = None if k else sheet
        slot = jnp.where(side == 0, own - 1 - k, k)
        maps = [lambda row, n, ref=ref: ref[slot, pl.ds(row, n), :] for ref in (far_cosine, far_sine)]
        propagate(plan, *maps, left, entering, ky, kz, km, field, spread)

    def step(k, left):
        entering = None
        slot = jnp.where(side == 0, 2 * own - 1 - k, k - own)
        maps = [lambda row, n, ref=ref: ref[slot, pl.ds(row, n), :] for ref in (cosine, sine)]
        propagate(plan, *maps, left, entering, ky, kz, km, field, spread)
        out[slot] = earlier[slot] + energy(plan, field)

    for k in range(own):
        far_step(k, 2 * own - 1 - k)
    for copy in arriving:
        copy.wait()
    for k in range(own, 2 * own):
        step(k, 2 * own - 1 - k)


def weight_kernel(plan, hbm_bright, hbm_labels, hbm_dtaps, facing, beyond, weight, by, bz, bright, labels, dtaps, line, sems):
    half, ny, cz = plan.half, plan.ny, plan.cz
    first, taps, arriving = fetch([(hbm_bright, bright), (hbm_dtaps, dtaps), (hbm_labels, labels)], sems)
    first.wait()
    taps.wait()
    padded, folded = tap_rows(ny, line)
    keep(by, circulant(folded(dtaps[0:1, :]), ny, half))
    keep(bz, band(padded(dtaps[1:2, :])[:, :2 * plan.block], plan.block, 2 * plan.block))
    tile = lax.axis_index("tile")
    even = lax.rem(tile, 2) == 0
    first_half = lax.broadcasted_iota(jnp.int32, (ny, 2 * half), 1) < half
    ends = [(tile < plan.tiles - 1).astype(jnp.float32), (tile > 0).astype(jnp.float32)]
    inside = jnp.where(first_half, ends[0], ends[1])
    values = [bright[e] for e in range(bright.shape[0])]
    for x in range(plan.planes):
        before = jnp.where(even, beyond[x], facing[x])[:, -2 * half:]
        behind = jnp.where(even, facing[x], beyond[x])[:, :2 * half]
        halo = (choose(jnp.where(first_half, behind, before), values)[0] * inside).T
        weight[x, :half, :] = halo[half:]
        weight[x, half + cz:, :] = halo[:half]
    arriving.wait()
    for x in range(plan.planes):
        weight[x, half:half + cz, :] = choose(labels[x], values)[0].T


def blur_kernel(plan, mine, other, weight, by, bz, out):
    ny, extent, block = plan.ny, plan.extent, plan.block
    parts = [(mine[x] + other[x]) * weight[x] for x in range(plan.planes)]
    high, low = halves(jnp.concatenate(parts, axis=0))
    v = three(high, low, by[0], by[1])
    v = jnp.concatenate([v[x * extent:(x + 1) * extent] for x in range(plan.planes)], axis=1)
    high, low = halves(v)
    for b in range(plan.cz // block):
        rows = slice(b * block, b * block + 2 * block)
        w = dot(bz[0], high[rows]) + dot(bz[1], high[rows]) + dot(bz[0], low[rows])
        for x in range(plan.planes):
            out[x, :, b * block:(b + 1) * block] = w[:, x * ny:(x + 1) * ny].T


def size_of(x):
    return x.size * x.dtype.itemsize


def call(kernel, outs, in_spaces, scratch=(), flops=0, out_spaces=None):
    return lambda *args: call_with(args, kernel, outs, in_spaces, scratch, flops, out_spaces)


def call_with(args, kernel, outs, in_spaces, scratch, flops, out_spaces):
    args = [
        pltpu.with_memory_space_constraint(x, space) if space is HBM or size_of(x) > PIN else x
        for x, space in zip(args, in_spaces)
    ]
    held = [x for x, space in zip(args, in_spaces) if space is VMEM]
    held += jax.tree.leaves(outs)
    held += [jax.ShapeDtypeStruct(x.shape, x.dtype) for x in scratch if x.memory_space == VMEM]
    if out_spaces is None:
        out_spaces = jax.tree.map(lambda _: VMEM, outs)
    limit = ROOM + sum(size_of(x) for x in held)
    flat, tree = jax.tree.flatten(outs)
    spaces = jax.tree.leaves(out_spaces)
    outs = tree.unflatten(
        [HBM(x.shape, x.dtype) if space is HBM else x for x, space in zip(flat, spaces)]
    )
    return pl.pallas_call(
        kernel,
        out_shape=outs,
        in_specs=[pl.BlockSpec(memory_space=space) for space in in_spaces],
        out_specs=jax.tree.map(lambda space: pl.BlockSpec(memory_space=space), out_spaces),
        scratch_shapes=list(scratch),
        compiler_params=pltpu.CompilerParams(vmem_limit_bytes=limit),
        cost_estimate=pl.CostEstimate(flops=flops, bytes_accessed=1 << 20, transcendentals=0),
    )(*args)


def on_device(labels, classes, positions, phase_table, brightness, prop_taps, detect_taps):
    taps = prop_taps.shape[-1]
    plan = Plan(labels, positions.shape[0], taps)
    ny, half, block, rows = plan.ny, plan.half, plan.block, plan.rows
    tiles, cores = plan.tiles, plan.cores
    core = plan.here()[2]
    f32, bf16 = jnp.float32, jnp.bfloat16
    shape = jax.ShapeDtypeStruct

    def over_cores(array):
        return [array] + [swap(array, "sect", bits) for bits in range(1, cores)]

    crossed = [swap(classes, "sect", cores)]
    pieces, sources = tile_pieces(plan, classes, crossed)
    near = [over_cores(piece) for piece in pieces]
    joined = [after(pieces[1], *near[1][1:]), *pieces[2:-1]]
    near_groups = tuple((source,) for source in sources)
    far_groups = (sources[:1], sources[1:-1], sources[-1:])
    line = -(-max(4 * half, taps) // ny) * ny
    phases = phase_table[None]
    ky, kz, km, table, sheet, together = call(
        functools.partial(prepare_kernel, plan, len(joined)),
        (
            shape((2, 2 * ny, 2 * ny), bf16),
            shape((2, 2, 2 * block, 2 * block), bf16),
            shape((2, 2 * block, 2 * block), bf16),
            shape((2 * phases.shape[1], ny), f32),
            shape((1, plan.width), f32),
            shape((len(joined) * plan.planes, ny, plan.cz), classes.dtype),
        ),
        [HBM] * 3 + [VMEM] * len(joined),
        [
            pltpu.VMEM(prop_taps.shape, f32),
            pltpu.VMEM(phases.shape, f32),
            pltpu.SMEM(positions.shape, positions.dtype),
            pltpu.VMEM((8, line), f32),
            pltpu.SemaphoreType.DMA((3,)),
        ],
    )(prop_taps, phases, positions, *joined)
    near = sum(near, [])
    crossed += [swap(together, "sect", cores), swap(pieces[-1], "sect", cores)]

    maps = shape((plan.own, rows, ny), f32)
    whole_maps = pltpu.VMEM((plan.own, rows, ny), f32)
    state = pltpu.VMEM((2, rows + 2 * half, plan.width), f32)
    sums = shape((plan.own, plan.extent, ny), f32)
    sums, cosine, sine = call(
        functools.partial(short_kernel, plan, near_groups),
        (sums, maps, maps),
        [VMEM] * (5 + len(near)),
        [
            whole_maps,
            whole_maps,
            state,
            state,
            pltpu.SemaphoreType.DMA((2,)),
        ],
        flops=1,
        out_spaces=(VMEM, HBM, HBM),
    )(near[0], ky, kz, km, table, sheet, *near[1:])

    pairs = [(i, i ^ 1) for i in range(tiles) if i ^ 1 < tiles]
    gaps = [(i, ((i + 1) ^ 1) - 1) for i in range(1, tiles) if ((i + 1) ^ 1) - 1 < tiles]
    if tiles == 4:
        gaps = [(i, i ^ 3) for i in range(tiles)]
    late = after(labels, sums)
    facing = lax.ppermute(late, "tile", pairs)
    beyond = lax.ppermute(late, "tile", gaps)

    far = []
    for piece in crossed:
        far += [piece] + over_cores(after(piece, sums))[1:]
    sums = call(
        functools.partial(long_kernel, plan, far_groups),
        shape((plan.own, plan.extent, ny), f32),
        [VMEM] * 5 + [HBM] * 2 + [VMEM] * (1 + len(far)),
        [whole_maps] * 4 + [state, state, pltpu.SemaphoreType.DMA((2,))],
        flops=6 * 10**9,
    )(ky, kz, km, table, sheet, cosine, sine, sums, *far)

    parts = sums.reshape(cores, plan.planes, plan.extent, ny)
    mine = lax.dynamic_index_in_dim(parts, core, 0, keepdims=False)
    other = None
    for bits in range(1, cores):
        leaving = lax.dynamic_index_in_dim(parts, core ^ bits, 0, keepdims=False)
        arrived = swap(after(leaving, facing, beyond), "sect", bits)
        other = arrived if other is None else other + arrived
    other = jnp.zeros_like(mine) if other is None else other
    weight, by, bz = call(
        functools.partial(weight_kernel, plan),
        (
            shape((plan.planes, plan.extent, ny), f32),
            shape((2, ny, ny), bf16),
            shape((2, block, 2 * block), bf16),
        ),
        [HBM] * 3 + [VMEM] * 2,
        [
            pltpu.SMEM(brightness.shape, f32),
            pltpu.VMEM(labels.shape, labels.dtype),
            pltpu.VMEM(detect_taps.shape, f32),
            pltpu.VMEM((8, line), f32),
            pltpu.SemaphoreType.DMA((3,)),
        ],
    )(brightness, labels, detect_taps, facing, beyond)
    return call(
        functools.partial(blur_kernel, plan),
        shape((plan.planes, ny, plan.cz), f32),
        [VMEM] * 5,
    )(mine, other, weight, by, bz)


def solution(mesh):
    spread = P(("groups", "sect"), None, "tile")
    in_specs = (spread, spread, P("groups"), P(), P(), P(), P())
    return jax.shard_map(
        on_device, mesh=mesh, in_specs=in_specs, out_specs=spread, check_vma=False
    )
```
